256 devices in a mesh: section: 16 (over z, y_hi), dp: 16 (over y_lo, x, core).
Axes of the slice: x: 4, y: 4 (y_hi: 2, y_lo: 2; y = y_hi * 2 + y_lo), z: 8, core: 2. Of those that a mesh axis runs over, the one named last changes fastest.
Arguments:
- context: bfloat16 [16, 2048, 6144], P('section', 'dp'), may hold values from -6 to 6
- back_terms: bfloat16 [16, 2048, 6144], P('section', 'dp'), may hold values from -3 to 3
- top_grad: bfloat16 [2048, 6144], P('dp'), may hold values from -6 to 6
- token_batch: int32 [2048], P('dp'), may hold values from 0 to 7
- plan: int32 [8], replicated, may hold values from 0 to 7, each once
Outputs:
- precond: bfloat16 [16, 6144, 6144], P('section', 'dp')
The draws below stay inside these ranges and needn't reach their ends.
Inputs may be any that keep to these rules, and one draw needn't show every extreme that they name: `plan`: each micro-batch appears exactly once.
All inputs are finite; a program needn't handle non-finite values.
Results may differ from the reference program's by a relative error of at most 0.02.
Values may be sent and summed in bfloat16 or wider, within the bound.
A program may use at most 256 MiB of HBM per device.

```python
import jax
import jax.numpy as jnp
from jax import lax

D = 6144
BLK = 384
MB = 8
TOKENS = 2048
SECTIONS = 16


def set_ends(array, rng, smallest, largest):
    dims = array.shape
    place = [jax.random.randint(jax.random.fold_in(rng, axis), (), 0, dims[axis]) for axis in range(len(dims))]
    array = array.at[tuple(place)].set(smallest)
    longest = dims.index(max(dims))
    place[longest] = (place[longest] + 1) % dims[longest]
    return array.at[tuple(place)].set(largest)


def levels(own_key, dims, split, least, top_value):
    loudness, own = 1.0, jax.random.fold_in(own_key, 6)
    for position, parts in split:
        heights = jnp.exp(jax.random.uniform(jax.random.fold_in(own, position), (parts,), jnp.float32, least / len(split), top_value / len(split)))
        loudness = loudness * jnp.repeat(heights, dims[position] // parts).reshape([-1 if axis == position else 1 for axis in range(len(dims))])
    return loudness


def gaussian(rng, shape, width, limit, pieces=(), kind=jnp.bfloat16):
    gain = levels(rng, shape, pieces, -0.22, 0.18) if pieces else 1.0
    array = jax.random.normal(rng, shape, jnp.float32) * width * gain
    return jnp.minimum(jnp.maximum(array, -limit), limit).astype(kind)


def setup_inputs(seed: int = 0) -> dict:
    streams_of = jax.random.split(jax.random.key(seed), 6)
    return {
        "context": gaussian(streams_of[0], (SECTIONS, TOKENS, D), 1.0, 6.0, ((0, 16), (1, 16))),
        "back_terms": gaussian(streams_of[1], (SECTIONS, TOKENS, D), 0.5, 3.0, ((0, 16), (1, 16))),
        "top_grad": gaussian(streams_of[2], (TOKENS, D), 1.0, 6.0, ((0, 16),)),
        "token_batch": set_ends(jax.random.randint(streams_of[3], (TOKENS,), 0, MB), jax.random.fold_in(streams_of[3], 1), 0, MB - 1).astype(jnp.int32),
        "plan": jax.random.permutation(streams_of[4], MB).astype(jnp.int32),
    }


falloff = 0.5
damping = 0.1

def token_weights(token_batch, plan):
    batch_slots = jnp.arange(MB, dtype=jnp.int32)
    lateness = (MB - 1 - plan).astype(jnp.float32)
    table = jnp.power(jnp.asarray(falloff, jnp.float32), lateness)
    matches = (token_batch[:, None] == batch_slots[None, :]).astype(jnp.float32)
    return jnp.sum(matches * table[None, :], axis=1)

def block_products(left_rows, right_rows):
    row_total = left_rows.shape[0]
    block_count = left_rows.shape[1] // BLK
    left_three = left_rows.reshape(row_total, block_count, BLK).astype(jnp.float32)
    right_three = right_rows.reshape(row_total, block_count, BLK).astype(jnp.float32)
    return jnp.einsum('tbi,tbj->bij', left_three, right_three)

def solve_block(chol_block, rhs_block):
    return jax.scipy.linalg.cho_solve((chol_block, True), rhs_block)

def section_result(ctx_rows, grad_full, weights):
    identity_blk = jnp.eye(BLK, dtype=jnp.float32)
    block_count = D // BLK
    weighted_ctx = (ctx_rows.astype(jnp.float32) * weights[:, None]).astype(jnp.bfloat16)
    weighted_grad = (grad_full.astype(jnp.float32) * weights[:, None]).astype(jnp.bfloat16)
    act_factor = block_products(weighted_ctx, ctx_rows) / TOKENS
    grad_factor = block_products(weighted_grad, grad_full) / TOKENS
    chol_grad = jnp.linalg.cholesky(grad_factor + damping * identity_blk)
    eyes = jnp.broadcast_to(identity_blk, (block_count, BLK, BLK))
    inverses = jax.vmap(solve_block)(chol_grad, eyes).astype(jnp.bfloat16)
    grad_three = grad_full.reshape(TOKENS, block_count, BLK).astype(jnp.float32)
    grad_pre = jnp.einsum('tck,ckj->tcj', grad_three, inverses.astype(jnp.float32))
    grad_pre = grad_pre.reshape(TOKENS, D).astype(jnp.bfloat16)
    summed = jnp.dot(ctx_rows.T.astype(jnp.float32), grad_pre.astype(jnp.float32), preferred_element_type=jnp.float32)
    row_grads = (summed / TOKENS).astype(jnp.bfloat16)
    chol_act = jnp.linalg.cholesky(act_factor + damping * identity_blk)
    rhs = row_grads.astype(jnp.float32).reshape(block_count, BLK, D)
    left_part = jax.vmap(solve_block)(chol_act, rhs)
    return left_part.reshape(D, D).astype(jnp.bfloat16)

def reference(context, back_terms, top_grad, token_batch, plan):
    weights = token_weights(token_batch, plan)
    top_float = top_grad.astype(jnp.float32)

    def per_section(carried, pair):
        ctx_rows, back_rows = pair
        residual_grad = (top_float + carried).astype(jnp.bfloat16)
        result = section_result(ctx_rows, residual_grad, weights)
        return (carried + back_rows.astype(jnp.float32), result)
    start_sum = jnp.zeros((TOKENS, D), jnp.float32)
    _, outputs = lax.scan(per_section, start_sum, (context, back_terms), reverse=True)
    return outputs
```

```python
import functools

import jax
import jax.numpy as jnp
from jax import lax
from jax.experimental import pallas as pl
from jax.experimental.pallas import tpu as pltpu
from jax.sharding import PartitionSpec as P

BLK = 384
MB = 8
MESH = pl.DeviceIdType.MESH
MIB = 1 << 20

falloff = 0.5
damping = 0.1


def columns(block):
    return pl.ds(pl.multiple_of(block * BLK, BLK), BLK)


ROW_PARTS = 4
W_ROWS = 16

ORDER_X = (1, 3, 2, 0, 3, 1, 2, 0)
ORDER_Y = (0, 1, 0, 1, 0, 1, 1, 0)
CODE_ORDER_X = sum(v << (2 * p) for p, v in enumerate(ORDER_X))
CODE_ORDER_Y = sum(v << p for p, v in enumerate(ORDER_Y))


def neighbour(d, dy, dx, dc):
    y, x, c = d // 8, lax.rem(d // 2, 4), lax.rem(d, 2)
    return lax.rem(y + dy, 2) * 8 + lax.rem(x + dx, 4) * 2 + lax.rem(c + dc, 2)


def in_turn(d, j):
    q = lax.rem(j, 8)
    dx = lax.shift_right_logical(jnp.int32(CODE_ORDER_X), 2 * q) & 3
    dy = lax.shift_right_logical(jnp.int32(CODE_ORDER_Y), q) & 1
    return neighbour(d, dy, dx, 1 - j // 8)


def suffix_kernel(
    sections, owners,
    back_hbm, top_hbm, ctx_ref, batch_ref, plan_ref,
    owned,
    back_ref, top_ref, w_ref, bufs,
    chain_send, chain_recv, pair_send, pair_recv, same_send, same_recv,
    ctx_send, ctx_recv, w_send, w_recv, own_sem,
):
    s = lax.axis_index("section")
    d = lax.axis_index("dp")
    z, h = s // 2, s % 2
    levels = sections // 2
    below = lax.rem(s + sections - 2, sections)
    above = lax.rem(s + 2, sections)
    pair = s + 1 - 2 * h
    size = back_ref.shape[0] // ROW_PARTS
    steps = owners * ROW_PARTS
    last = owners - 1

    loads = [
        pltpu.make_async_copy(back_hbm, back_ref, own_sem.at[0]),
        pltpu.make_async_copy(top_hbm, top_ref, own_sem.at[1]),
    ]
    for load in loads:
        load.start()

    barrier = pltpu.get_barrier_semaphore()
    for other in (below, above):
        pl.semaphore_signal(barrier, inc=1, device_id={"section": other}, device_id_type=MESH)

    @pl.loop(0, owners)
    def _(j):
        pl.semaphore_signal(barrier, inc=1, device_id={"section": pair, "dp": j}, device_id_type=MESH)

        @pl.when(j > 0)
        def _():
            pl.semaphore_signal(barrier, inc=1, device_id={"dp": lax.rem(d + j, owners)}, device_id_type=MESH)

    weight = jnp.zeros(batch_ref.shape, jnp.float32)
    for slot in range(MB):
        late = MB - 1 - plan_ref[slot]
        value = jnp.float32(1.0)
        for bit in range(3):
            value = value * jnp.where((late & (1 << bit)) != 0, jnp.float32(falloff ** (1 << bit)), jnp.float32(1.0))
        weight = jnp.where(batch_ref[...] == slot, value, weight)
    w_ref[...] = jnp.broadcast_to(weight, w_ref.shape).astype(w_ref.dtype)

    @pl.when(z == levels - 1)
    def _():
        @pl.loop(0, owners)
        def _(j):
            bufs[0, j] = jnp.zeros(bufs.shape[2:], bufs.dtype)

    pl.semaphore_wait(barrier, 2 * owners + 1)

    every_row = pl.ds(0, back_ref.shape[0])
    rows_of_ctx = owned.at[2, d, every_row]
    rows_of_w = owned.at[2, d, pl.ds(back_ref.shape[0], w_ref.shape[0]), pl.ds(0, w_ref.shape[1])]

    def ctx_copy(j):
        to = in_turn(d, j)
        return pltpu.make_async_remote_copy(
            src_ref=ctx_ref.at[:, columns(to)], dst_ref=rows_of_ctx,
            send_sem=ctx_send.at[j], recv_sem=ctx_recv.at[j],
            device_id={"dp": to}, device_id_type=MESH)

    def w_copy(j):
        to = in_turn(d, j)
        return pltpu.make_async_remote_copy(
            src_ref=w_ref, dst_ref=rows_of_w,
            send_sem=w_send.at[j], recv_sem=w_recv.at[j],
            device_id={"dp": to}, device_id_type=MESH)

    def chain_copy(j, part):
        i, rows = j * ROW_PARTS + part, pl.ds(part * size, size)
        return pltpu.make_async_remote_copy(
            src_ref=bufs.at[1, j, rows], dst_ref=bufs.at[0, j, rows],
            send_sem=chain_send.at[i], recv_sem=chain_recv.at[i],
            device_id={"section": below}, device_id_type=MESH)

    def pair_copy(j, to):
        return pltpu.make_async_remote_copy(
            src_ref=bufs.at[2 - h, j], dst_ref=owned.at[h, d, every_row],
            send_sem=pair_send.at[j], recv_sem=pair_recv.at[j],
            device_id={"section": pair, "dp": to}, device_id_type=MESH)

    def same_copy(j, to):
        return pltpu.make_async_remote_copy(
            src_ref=bufs.at[2 - 2 * h, j], dst_ref=owned.at[h, d, every_row],
            send_sem=same_send.at[j], recv_sem=same_recv.at[j],
            device_id={"dp": to}, device_id_type=MESH)

    own_ctx = pltpu.make_async_copy(ctx_ref.at[:, columns(d)], rows_of_ctx, own_sem.at[2])
    own_w = pltpu.make_async_copy(w_ref, rows_of_w, own_sem.at[3])
    own_part = pltpu.make_async_copy(bufs.at[2 - 2 * h, last], owned.at[h, d, every_row], own_sem.at[4])
    own_ctx.start()
    own_w.start()

    early = z < levels - 1

    @pl.when(early)
    def _():
        @pl.loop(0, last)
        def _(j):
            w_copy(j).start()
            ctx_copy(j).start()

    for load in loads:
        load.wait()

    @pl.loop(0, owners)
    def _(j):
        to = in_turn(d, j)
        cols = columns(to)
        for part in range(ROW_PARTS):
            rows = pl.ds(part * size, size)

            @pl.when(z < levels - 1)
            def _():
                chain_copy(j, part).wait_recv()

            came = bufs[0, j, rows, :].astype(jnp.float32)
            bufs[1, j, rows, :] = (came + back_ref[rows, cols].astype(jnp.float32)).astype(jnp.bfloat16)

            @pl.when(z > 0)
            def _():
                chain_copy(j, part).start()

        @pl.when(h == 0)
        def _():
            bufs[2, j] = (bufs[0, j].astype(jnp.float32) + top_ref[:, cols].astype(jnp.float32)).astype(jnp.bfloat16)

        pair_copy(j, to).start()

        @pl.when(j < last)
        def _():
            same_copy(j, to).start()

        @pl.when(jnp.logical_not(early) & (j < last))
        def _():
            w_copy(j).start()
            ctx_copy(j).start()

    own_part.start()

    @pl.loop(0, owners)
    def _(j):
        @pl.when(z > 0)
        def _():
            for part in range(ROW_PARTS):
                chain_copy(j, part).wait_send()

        pair_copy(j, d).wait()

        @pl.when(j < last)
        def _():
            same_copy(j, in_turn(d, j)).wait()

    @pl.loop(0, last)
    def _(j):
        w_copy(j).wait()
        ctx_copy(j).wait()

    for copy in (own_ctx, own_w, own_part):
        copy.wait()


def suffix_and_columns(back, top, ctx, token_batch, plan, sections, owners):
    rows, width = ctx.shape
    chunk = (owners, rows, BLK)
    dma = pltpu.SemaphoreType.DMA
    steps = owners * ROW_PARTS
    return pl.pallas_call(
        functools.partial(suffix_kernel, sections, owners),
        out_shape=jax.ShapeDtypeStruct((3, owners, rows + W_ROWS, BLK), jnp.bfloat16),
        in_specs=[pl.BlockSpec(memory_space=pltpu.HBM)] * 3 + [
            pl.BlockSpec(memory_space=pltpu.VMEM),
            pl.BlockSpec(memory_space=pltpu.SMEM),
        ],
        out_specs=pl.BlockSpec(memory_space=pl.ANY),
        scratch_shapes=[
            pltpu.VMEM((rows, width), jnp.bfloat16),
            pltpu.VMEM((rows, width), jnp.bfloat16),
            pltpu.VMEM((W_ROWS, rows), jnp.bfloat16),
            pltpu.VMEM((3,) + chunk, jnp.bfloat16),
        ] + [dma((steps,))] * 2 + [dma((owners,))] * 8 + [dma((5,))],
        compiler_params=pltpu.CompilerParams(
            collective_id=0, has_side_effects=True, vmem_limit_bytes=54 * MIB),
        cost_estimate=pl.CostEstimate(flops=10 ** 7, bytes_accessed=10 ** 7, transcendentals=0),
    )(back, top, ctx, token_batch.reshape(1, rows), plan)


def split(x):
    high = x.astype(jnp.bfloat16)
    return high, (x - high.astype(jnp.float32)).astype(jnp.bfloat16)


def mm(a, b):
    return jnp.dot(a, b, preferred_element_type=jnp.float32)


PIECES = 4


def eye_block():
    rows = lax.broadcasted_iota(jnp.int32, (BLK, BLK), 0)
    return (rows == lax.broadcasted_iota(jnp.int32, (BLK, BLK), 1)).astype(jnp.float32)


def spectrum(squared):
    sums = jnp.sum(jnp.abs(squared), axis=0, keepdims=True)
    return jnp.sqrt(jnp.max(sums, axis=1, keepdims=True)) * 1.001


def first_steps(a, squared):
    top = spectrum(squared)
    reach = (top - damping) / (top + damping)
    scale = 2.0 / (top + damping)
    grow = 2.0 / (2.0 - reach * reach)
    eye = eye_block()
    inv = grow * (2.0 * scale * eye - (scale * scale) * a)
    residual = eye - grow * (2.0 * scale * a - (scale * scale) * squared)
    return inv, residual, after(reach)


def after(reach):
    return reach * reach / (2.0 - reach * reach)


def exact(a, b):
    return jnp.dot(a, b, precision=lax.Precision.HIGHEST, preferred_element_type=jnp.float32)


def inverse_kernel(
    tokens, owned, pre_ref,
    parts_ref, w_ref, grad_ref, weighted, mat, inv, mat_left, inv_left, inv_right, twice, sems,
):
    _, owners, tile, _ = parts_ref.shape
    eye = eye_block()
    piece = owners // PIECES
    loads = []
    for k in range(PIECES):
        some = pl.ds(k * piece, piece)
        loads.append((
            pltpu.make_async_copy(
                owned.at[pl.ds(0, 2), some, pl.ds(0, tile)], parts_ref.at[:, some], sems.at[0, k]),
            pltpu.make_async_copy(
                owned.at[2, some, pl.ds(tile, W_ROWS), pl.ds(0, tile)], w_ref.at[some], sems.at[1, k]),
        ))
        for load in loads[-1]:
            load.start()

    def turn(t):
        at = pl.ds(t * tile, tile)
        w = w_ref[t, 0:1, :].astype(jnp.float32)
        grad = parts_ref[0, t].astype(jnp.float32) + parts_ref[1, t].astype(jnp.float32)
        grad = grad.astype(jnp.bfloat16)
        grad_ref[at, :] = grad
        weighted[:, at] = (grad.astype(jnp.float32).T * w).astype(jnp.bfloat16)

    for k in range(PIECES):
        for load in loads[k]:
            load.wait()
        for t in range(k * piece, (k + 1) * piece):
            turn(t)

    def put_right(high, low):
        inv_right[0:BLK, :] = high
        inv_right[BLK:2 * BLK, :] = low
        inv_right[2 * BLK:3 * BLK, :] = high

    def put_inverse(x):
        inv[...] = x
        high, low = split(x)
        put_right(high, low)
        inv_left[:, 0:BLK] = high
        inv_left[:, BLK:2 * BLK] = low

    def put_residual(residual):
        residual = residual.astype(jnp.bfloat16)
        twice[0:BLK, :] = residual
        twice[BLK:2 * BLK, :] = residual

    a = mm(weighted[...], grad_ref[...]) * (1.0 / tokens) + damping * eye
    mat[...] = a
    high, low = split(a)
    mat_left[:, 0:BLK] = high
    mat_left[:, BLK:2 * BLK] = high
    mat_left[:, 2 * BLK:3 * BLK] = low
    put_right(high, low)
    squared = mm(mat_left[...], inv_right[...])
    x, residual, reach = first_steps(a, squared)
    put_inverse(x)
    put_residual(residual)
    reach = jnp.max(reach)
    quick = jnp.max(spectrum(squared)) <= 512.0 * damping

    def quick_update(reach):
        step = mm(inv_left[...], twice[...])
        put_inverse((2.0 / (2.0 - reach * reach)) * (inv[...] + step))
        return after(reach)

    def quick_body(reach):
        put_residual(eye - mm(mat_left[...], inv_right[...]))
        return quick_update(reach)

    def full_body(reach):
        x = inv[...]
        inv[...] = (2.0 / (2.0 - reach * reach)) * (x + exact(x, eye - exact(mat[...], x)))
        return after(reach)

    @pl.when(quick)
    def _():
        lax.while_loop(lambda r: r > 1e-4, quick_body, quick_update(reach))

    @pl.when(jnp.logical_not(quick))
    def _():
        lax.while_loop(lambda r: r > 1e-6, full_body, reach)

    pre_ref[...] = mm(grad_ref[...], inv[...].astype(jnp.bfloat16)).astype(jnp.bfloat16)


def inverses(owned):
    _, owners, tile, _ = owned.shape
    tile = tile - W_ROWS
    tokens = owners * tile
    square = (BLK, BLK)
    return pl.pallas_call(
        functools.partial(inverse_kernel, tokens),
        out_shape=jax.ShapeDtypeStruct((tokens, BLK), jnp.bfloat16),
        in_specs=[pl.BlockSpec(memory_space=pl.ANY)],
        out_specs=pl.BlockSpec(memory_space=pltpu.VMEM),
        scratch_shapes=[
            pltpu.VMEM((2, owners, tile, BLK), jnp.bfloat16),
            pltpu.VMEM((owners, W_ROWS, tile), jnp.bfloat16),
            pltpu.VMEM((tokens, BLK), jnp.bfloat16),
            pltpu.VMEM((BLK, tokens), jnp.bfloat16),
            pltpu.VMEM(square, jnp.float32),
            pltpu.VMEM(square, jnp.float32),
            pltpu.VMEM((BLK, 3 * BLK), jnp.bfloat16),
            pltpu.VMEM((BLK, 2 * BLK), jnp.bfloat16),
            pltpu.VMEM((3 * BLK, BLK), jnp.bfloat16),
            pltpu.VMEM((2 * BLK, BLK), jnp.bfloat16),
            pltpu.SemaphoreType.DMA((2, PIECES)),
        ],
        compiler_params=pltpu.CompilerParams(vmem_limit_bytes=48 * MIB),
        cost_estimate=pl.CostEstimate(flops=2 * 10 ** 10, bytes_accessed=10 ** 7, transcendentals=0),
    )(owned)


DX = (0, 1, 3, 0, 2, 1, 3, 2)
DY = (0, 0, 0, 1, 0, 1, 1, 1)
CODE_X = sum(v << (2 * p) for p, v in enumerate(DX))
CODE_Y = sum(v << p for p, v in enumerate(DY))


def newton_steps(largest, goal):
    reach, steps = (largest - damping) / (largest + damping), 0
    while reach > goal:
        reach, steps = reach * reach / (2.0 - reach * reach), steps + 1
    return steps


INPUT_STEPS = newton_steps((BLK * 36.0 + damping) * 1.01, 1e-4)


def gather_kernel(
    owners, tokens,
    pre_ref, owned, out_ref,
    held, done, begun, ctx_ref, w_ref, ctx_t, pt_ref, mat, inv,
    send_up, send_down, send_y, send_sib, recv, recv_sib, own_sem, out_sem,
):
    d = lax.axis_index("dp")
    half, part = tokens // 2, tokens // 16
    end, far, near = tokens // 96 * 16, 11 * part, 5 * part
    low, high = (0, half), (half, half)
    quarters = [(k * half // 2, half // 2) for k in range(4)]
    middles_5, tail = ((half, far - half), (far, tokens - end - far)), (tokens - end, end)
    middles_6, head = ((near, half - near), (end, near - end)), (0, end)

    def place(p, dc):
        if isinstance(p, int):
            return neighbour(d, DY[p], DX[p], dc)
        dx = lax.shift_right_logical(jnp.int32(CODE_X), 2 * p) & 3
        dy = lax.shift_right_logical(jnp.int32(CODE_Y), p) & 1
        return neighbour(d, dy, dx, dc)

    up, down = neighbour(d, 0, 1, 0), neighbour(d, 0, 3, 0)
    across, sibling = neighbour(d, 1, 0, 0), neighbour(d, 0, 0, 1)

    barrier = pltpu.get_barrier_semaphore()
    for other in (up, down, across, sibling):
        pl.semaphore_signal(barrier, inc=1, device_id={"dp": other}, device_id_type=MESH)
    own = pltpu.make_async_copy(pre_ref, held.at[d], own_sem.at[0])
    own.start()
    tile = ctx_ref.shape[1]
    loads = [
        pltpu.make_async_copy(owned.at[2, :, pl.ds(0, tile)], ctx_ref, own_sem.at[1]),
        pltpu.make_async_copy(owned.at[2, :, pl.ds(tile, W_ROWS), pl.ds(0, tile)], w_ref, own_sem.at[2]),
    ]
    for load in loads:
        load.start()
    pl.semaphore_wait(barrier, 4)

    started = []
    slot = {low: 0, high: 2, tail: 3, head: 3}
    slot.update((rows, k) for k, rows in enumerate(quarters))
    for middles in (middles_5, middles_6):
        slot.update(zip(middles, (1, 4)))
    count = {"up": 0, "down": 0, "across": 0}

    def send(p, part, to, send_sem, recv_sem):
        rows = pl.ds(*part)
        target = held.at[place(p, 0), rows]
        copy = pltpu.make_async_remote_copy(
            src_ref=pre_ref.at[rows] if p == 0 else target, dst_ref=target,
            send_sem=send_sem, recv_sem=recv_sem,
            device_id={"dp": to}, device_id_type=MESH)
        copy.start()
        started.append(copy)

    def pass_on(way, p, part, there):
        to, sems = {"up": (up, send_up), "down": (down, send_down), "across": (across, send_y)}[way]
        send(p, part, to, sems.at[count[way]], recv.at[there, slot[part]])
        count[way] += 1

    def to_sibling(p, part):
        send(p, part, sibling, send_sib.at[p, slot[part]], recv_sib.at[p, slot[part]])

    def arrived(p, part, dc=0):
        at = held.at[place(p, dc), pl.ds(*part)]
        sems = recv_sib if dc else recv
        pltpu.make_async_copy(at, at, sems.at[p, slot[part]]).wait()

    def got(p, part):
        arrived(p, part)
        to_sibling(p, part)

    def out_copy(block):
        return pltpu.make_async_copy(done.at[block], out_ref.at[:, columns(block)], out_sem.at[block])

    def finish(block, total):
        done[block] = total.astype(jnp.bfloat16)
        out_copy(block).start()

    def multiply(p, dc):
        block = place(p, dc)
        finish(block, mm(pt_ref[...], held[block]))

    def partial(p, dc, *spans):
        block = place(p, dc)
        return sum(mm(pt_ref[:, a:b], held[block, a:b, :]) for a, b in spans)

    def begin_multiply(p, dc, *spans):
        begun[2 * (p - 5) + dc] = partial(p, dc, *spans)

    def go_on(p, dc, *spans):
        begun[2 * (p - 5) + dc] += partial(p, dc, *spans)

    def end_multiply(p, dc, *spans):
        finish(place(p, dc), begun[2 * (p - 5) + dc] + partial(p, dc, *spans))

    for k in range(2):
        pass_on("up", 0, quarters[k], 2)
        pass_on("down", 0, quarters[2 + k], 1)
    pass_on("across", 0, low, 3)
    pass_on("across", 0, high, 3)
    to_sibling(0, low)
    to_sibling(0, high)
    own.wait()
    for load in loads:
        load.wait()

    @pl.loop(0, owners)
    def _(t):
        at = pl.ds(pl.multiple_of(t * tile, tile), tile)
        turned = ctx_ref[t].astype(jnp.float32).T
        ctx_t[:, at] = turned.astype(jnp.bfloat16)
        pt_ref[:, at] = (turned * w_ref[t, 0:1, :].astype(jnp.float32)).astype(jnp.bfloat16)

    eye = eye_block()
    mat[...] = mm(pt_ref[...], ctx_ref[...].reshape(tokens, BLK)) * (1.0 / tokens) + damping * eye
    x, residual, reach = first_steps(mat[...], exact(mat[...], mat[...]))
    inv[...] = (2.0 / (2.0 - reach * reach)) * (x + exact(x, residual))

    def newton(_, reach):
        x = inv[...]
        inv[...] = (2.0 / (2.0 - reach * reach)) * (x + exact(x, eye - exact(mat[...], x)))
        return after(reach)

    arrived(2, quarters[0])
    pass_on("up", 2, quarters[0], 4)
    arrived(1, quarters[2])
    pass_on("down", 1, quarters[2], 4)
    reach = lax.fori_loop(2, 4, newton, after(reach))
    arrived(2, quarters[1])
    pass_on("up", 2, quarters[1], 4)
    pass_on("up", 0, high, 2)
    arrived(1, quarters[3])
    pass_on("down", 1, quarters[3], 4)
    pass_on("down", 0, low, 1)
    pass_on("across", 1, tail, 5)
    pass_on("across", 2, head, 6)
    for k in range(2):
        to_sibling(2, quarters[k])
        to_sibling(1, quarters[2 + k])
    got(3, low)

    reach = lax.fori_loop(4, 8, newton, reach)
    for k in range(2):
        arrived(4, quarters[k])
        pass_on("across", 4, quarters[k], 7)
        arrived(4, quarters[2 + k])
        pass_on("across", 4, quarters[2 + k], 7)
    pass_on("down", 3, low, 5)
    arrived(3, high)
    pass_on("up", 3, high, 6)
    for k in range(2):
        pass_on("down", 3, middles_5[k], 5)
        pass_on("up", 3, middles_6[k], 6)
    to_sibling(3, high)
    for k in range(4):
        to_sibling(4, quarters[k])

    lax.fori_loop(8, INPUT_STEPS, newton, reach)
    ahead, behind = split(inv[...])
    rest_of_it = (inv[...] - ahead.astype(jnp.float32) - behind.astype(jnp.float32)).astype(jnp.bfloat16)
    pt_ref[...] = (
        mm(ahead, ctx_t[...]) + (mm(behind, ctx_t[...]) + mm(rest_of_it, ctx_t[...]))).astype(jnp.bfloat16)

    @pl.loop(0, 1)
    def _(p):
        multiply(p, 0)

    @pl.loop(3, 5)
    def _(p):
        multiply(p, 0)

    got(2, high)
    got(1, low)

    @pl.loop(1, 3)
    def _(p):
        multiply(p, 0)

    for rows in (low, high):
        arrived(0, rows, 1)
        arrived(3, rows, 1)
    for k in range(2):
        arrived(1, quarters[2 + k], 1)
        arrived(2, quarters[k], 1)
    for k in range(4):
        arrived(4, quarters[k], 1)
    arrived(1, low, 1)
    arrived(2, high, 1)

    @pl.loop(0, 5)
    def _(p):
        multiply(p, 1)

    got(5, tail)
    got(6, head)
    got(7, quarters[0])
    got(7, quarters[2])
    got(5, low)
    got(6, high)
    soon = (0, half // 2), (half, half + half // 2)
    late = (half // 2, half), (half + half // 2, tokens)
    for dc in range(2):
        if dc:
            arrived(7, quarters[0], 1)
            arrived(7, quarters[2], 1)
            arrived(5, low, 1)
            arrived(6, high, 1)
        begin_multiply(7, dc, *soon)
        begin_multiply(5, dc, (0, half))
        begin_multiply(6, dc, (half, tokens))

    got(5, middles_5[0])
    got(6, middles_6[0])
    for dc in range(2):
        if dc:
            arrived(5, tail, 1)
            arrived(6, head, 1)
            arrived(5, middles_5[0], 1)
            arrived(6, middles_6[0], 1)
        go_on(5, dc, (half, far), (tokens - 2 * part, tokens))
        go_on(6, dc, (near, half), (0, 2 * part))

    got(7, quarters[1])
    got(7, quarters[3])
    got(5, middles_5[1])
    got(6, middles_6[1])
    for dc in range(2):
        if dc:
            arrived(7, quarters[1], 1)
            arrived(7, quarters[3], 1)
            arrived(5, middles_5[1], 1)
            arrived(6, middles_6[1], 1)
        end_multiply(7, dc, *late)
        end_multiply(5, dc, (far, tokens - 2 * part))
        end_multiply(6, dc, (2 * part, near))

    for copy in started:
        copy.wait_send()

    @pl.loop(0, owners)
    def _(block):
        out_copy(block).wait()


def gather_and_multiply(pre, owned):
    tokens = pre.shape[0]
    _, owners, tile, _ = owned.shape
    tile = tile - W_ROWS
    dma = pltpu.SemaphoreType.DMA
    product = pl.pallas_call(
        functools.partial(gather_kernel, owners, tokens),
        out_shape=jax.ShapeDtypeStruct((BLK, owners * BLK), jnp.bfloat16),
        in_specs=[pl.BlockSpec(memory_space=pl.ANY)] * 2,
        out_specs=pl.BlockSpec(memory_space=pl.ANY),
        scratch_shapes=[
            pltpu.VMEM((owners, tokens, BLK), jnp.bfloat16),
            pltpu.VMEM((owners, BLK, BLK), jnp.bfloat16),
            pltpu.VMEM((6, BLK, BLK), jnp.float32),
            pltpu.VMEM((owners, tile, BLK), jnp.bfloat16),
            pltpu.VMEM((owners, W_ROWS, tile), jnp.bfloat16),
            pltpu.VMEM((BLK, tokens), jnp.bfloat16),
            pltpu.VMEM((BLK, tokens), jnp.bfloat16),
            pltpu.VMEM((BLK, BLK), jnp.float32),
            pltpu.VMEM((BLK, BLK), jnp.float32),
            dma((8,)), dma((8,)), dma((8,)), dma((8, 5)), dma((8, 5)), dma((8, 5)), dma((3,)), dma((owners,)),
        ],
        compiler_params=pltpu.CompilerParams(
            collective_id=1, has_side_effects=True, vmem_limit_bytes=46 * MIB),
        cost_estimate=pl.CostEstimate(flops=10 ** 10, bytes_accessed=10 ** 7, transcendentals=0),
    )(pre, owned)
    return product * jnp.bfloat16(1.0 / tokens)


def local(context, back_terms, top_grad, token_batch, plan):
    sections, owners = lax.axis_size("section"), lax.axis_size("dp")
    owned = suffix_and_columns(
        back_terms[0], top_grad, context[0], token_batch, plan, sections, owners)
    return gather_and_multiply(inverses(owned), owned)[None]


def solution(mesh):
    return jax.shard_map(
        local,
        mesh=mesh,
        in_specs=(P("section", "dp", None), P("section", "dp", None), P("dp", None), P("dp"), P()),
        out_specs=P("section", "dp", None),
        check_vma=False,
    )
```

```python
import functools

import jax
import jax.numpy as jnp
from jax import lax
from jax.experimental import pallas as pl
from jax.experimental.pallas import tpu as pltpu
from jax.sharding import PartitionSpec as P

BLK = 384
MB = 8
MESH = pl.DeviceIdType.MESH
MIB = 1 << 20

falloff = 0.5
damping = 0.1


def columns(block):
    return pl.ds(pl.multiple_of(block * BLK, BLK), BLK)


ROW_PARTS = 4
W_ROWS = 16

OTHER, SUM, NEXT, GRAD = 0, 1, 2, 3

ORDER_X = (1, 3, 2, 0, 3, 1, 2, 0)
ORDER_Y = (0, 1, 0, 1, 0, 1, 1, 0)
CODE_ORDER_X = sum(v << (2 * p) for p, v in enumerate(ORDER_X))
CODE_ORDER_Y = sum(v << p for p, v in enumerate(ORDER_Y))


def neighbour(d, dy, dx, dc):
    y, x, c = d // 8, lax.rem(d // 2, 4), lax.rem(d, 2)
    return lax.rem(y + dy, 2) * 8 + lax.rem(x + dx, 4) * 2 + lax.rem(c + dc, 2)


def in_turn(d, j):
    q = lax.rem(j, 8)
    dx = lax.shift_right_logical(jnp.int32(CODE_ORDER_X), 2 * q) & 3
    dy = lax.shift_right_logical(jnp.int32(CODE_ORDER_Y), q) & 1
    return neighbour(d, dy, dx, 1 - j // 8)


PARTNER_TURN = 8 + next(q for q in range(8) if (ORDER_X[q], ORDER_Y[q]) == (0, 1))


def over_y(j):
    return lax.shift_right_logical(jnp.int32(CODE_ORDER_Y), lax.rem(j, 8)) & 1


def suffix_kernel(
    sections, owners,
    back_hbm, top_hbm, ctx_ref, batch_ref, plan_ref,
    owned,
    back_ref, top_ref, w_ref, bufs,
    other_send, other_recv, chain_send, chain_recv, pair_send, pair_recv, same_send, same_recv,
    ctx_send, ctx_recv, w_send, w_recv, own_sem,
):
    s = lax.axis_index("section")
    d = lax.axis_index("dp")
    z, h = s // 2, s % 2
    levels = sections // 2
    below = lax.rem(s + sections - 2, sections)
    above = lax.rem(s + 2, sections)
    pair = s + 1 - 2 * h
    size = back_ref.shape[0] // ROW_PARTS
    blocks = owners // 2
    last = owners - 1

    loads = [
        pltpu.make_async_copy(back_hbm, back_ref, own_sem.at[0]),
        pltpu.make_async_copy(top_hbm, top_ref, own_sem.at[1]),
    ]
    for load in loads:
        load.start()

    barrier = pltpu.get_barrier_semaphore()
    for other in (below, above):
        pl.semaphore_signal(barrier, inc=1, device_id={"section": other}, device_id_type=MESH)

    @pl.loop(0, owners)
    def _(j):
        pl.semaphore_signal(barrier, inc=1, device_id={"section": pair, "dp": j}, device_id_type=MESH)

        @pl.when(j > 0)
        def _():
            pl.semaphore_signal(barrier, inc=1, device_id={"dp": lax.rem(d + j, owners)}, device_id_type=MESH)

    weight = jnp.zeros(batch_ref.shape, jnp.float32)
    for slot in range(MB):
        late = MB - 1 - plan_ref[slot]
        value = jnp.float32(1.0)
        for bit in range(3):
            value = value * jnp.where((late & (1 << bit)) != 0, jnp.float32(falloff ** (1 << bit)), jnp.float32(1.0))
        weight = jnp.where(batch_ref[...] == slot, value, weight)
    w_ref[...] = jnp.broadcast_to(weight, w_ref.shape).astype(w_ref.dtype)

    @pl.when(z == levels - 1)
    def _():
        @pl.loop(0, blocks)
        def _(j):
            bufs[SUM, j] = jnp.zeros(bufs.shape[2:], bufs.dtype)

    pl.semaphore_wait(barrier, 2 * owners + 1)

    every_row = pl.ds(0, back_ref.shape[0])
    rows_of_grad = owned.at[0, d, every_row]
    rows_of_ctx = owned.at[1, d, every_row]
    rows_to_pass = owned.at[2, d, every_row]
    rows_of_w = owned.at[1, d, pl.ds(back_ref.shape[0], w_ref.shape[0]), pl.ds(0, w_ref.shape[1])]

    across = neighbour(d, 1, 0, 0)

    def ctx_copy(j):
        to, dy = in_turn(d, j), over_y(j)
        return pltpu.make_async_remote_copy(
            src_ref=ctx_ref.at[:, columns(to)], dst_ref=owned.at[1 + dy, d, every_row],
            send_sem=ctx_send.at[j], recv_sem=ctx_recv.at[j],
            device_id={"dp": neighbour(to, dy, 0, 0)}, device_id_type=MESH)

    def w_copy(j):
        to = in_turn(d, j)
        return pltpu.make_async_remote_copy(
            src_ref=w_ref, dst_ref=rows_of_w,
            send_sem=w_send.at[j], recv_sem=w_recv.at[j],
            device_id={"dp": to}, device_id_type=MESH)

    def owner(i, mine):
        core = 1 - h if mine else h
        if isinstance(i, int):
            return neighbour(d, ORDER_Y[i], ORDER_X[i], core)
        return in_turn(d, i + blocks * (1 - core))

    def other_copy(i):
        return pltpu.make_async_remote_copy(
            src_ref=back_hbm.at[:, columns(owner(i, False))], dst_ref=bufs.at[OTHER, i],
            send_sem=other_send.at[i], recv_sem=other_recv.at[i],
            device_id={"section": pair}, device_id_type=MESH)

    def chain_copy(i, part):
        k, rows = i * ROW_PARTS + part, pl.ds(part * size, size)
        return pltpu.make_async_remote_copy(
            src_ref=bufs.at[NEXT, i, rows], dst_ref=bufs.at[SUM, i, rows],
            send_sem=chain_send.at[k], recv_sem=chain_recv.at[k],
            device_id={"section": below}, device_id_type=MESH)

    def pair_copy(i, to):
        return pltpu.make_async_remote_copy(
            src_ref=bufs.at[GRAD + 1 - h, i], dst_ref=rows_of_grad,
            send_sem=pair_send.at[i], recv_sem=pair_recv.at[i],
            device_id={"section": pair, "dp": to}, device_id_type=MESH)

    def same_copy(i, to):
        return pltpu.make_async_remote_copy(
            src_ref=bufs.at[GRAD + h, i], dst_ref=rows_of_grad,
            send_sem=same_send.at[i], recv_sem=same_recv.at[i],
            device_id={"dp": to}, device_id_type=MESH)

    def remote(i):
        return (h == 0) | (i < blocks - 1)

    own_ctx = pltpu.make_async_copy(ctx_ref.at[:, columns(d)], rows_of_ctx, own_sem.at[2])
    own_w = pltpu.make_async_copy(w_ref, rows_of_w, own_sem.at[3])
    own_grad = pltpu.make_async_copy(bufs.at[GRAD + 1, blocks - 1], rows_of_grad, own_sem.at[4])

    @pl.loop(0, blocks)
    def _(i):
        other_copy(i).start()

    own_pass = pltpu.make_async_copy(ctx_ref.at[:, columns(across)], rows_to_pass, own_sem.at[5])
    own_ctx.start()
    own_w.start()
    own_pass.start()

    def send_ctx(j):
        w_copy(j).start()

        if not isinstance(j, int):
            pl.when(j != PARTNER_TURN)(lambda: ctx_copy(j).start())
        elif j != PARTNER_TURN:
            ctx_copy(j).start()

    head = z == levels - 1

    @pl.when(jnp.logical_not(head))
    def _():
        pl.loop(0, last)(send_ctx)

    for load in loads:
        load.wait()

    upper = z >= levels // 2
    later = z - 1

    def finished(i):
        return jnp.clip(2 * (i - later), 0, i)

    def finish(i):
        to = owner(i, True)
        cols = columns(to)
        odd = bufs[SUM, i].astype(jnp.float32) + top_ref[:, cols].astype(jnp.float32)
        bufs[GRAD + 1, i] = odd.astype(jnp.bfloat16)

        @pl.when(h == 0)
        def _():
            bufs[GRAD, i] = (odd + bufs[OTHER, i].astype(jnp.float32)).astype(jnp.bfloat16)

        @pl.when(h == 1)
        def _():
            bufs[GRAD, i] = (odd + back_ref[:, cols].astype(jnp.float32)).astype(jnp.bfloat16)

        pair_copy(i, to).start()

        @pl.when(remote(i))
        def _():
            same_copy(i, to).start()

    for i in range(blocks):
        cols = columns(owner(i, True))
        other_copy(i).wait_recv()
        for part in range(ROW_PARTS):
            rows = pl.ds(part * size, size)

            @pl.when(z < levels - 1)
            def _():
                chain_copy(i, part).wait_recv()

            @pl.when(z > 0)
            def _():
                here = back_ref[rows, cols].astype(jnp.float32) + bufs[OTHER, i, rows, :].astype(jnp.float32)
                bufs[NEXT, i, rows, :] = (bufs[SUM, i, rows, :].astype(jnp.float32) + here).astype(jnp.bfloat16)
                chain_copy(i, part).start()

        @pl.when(head)
        def _():
            for j in range(2 * i, min(2 * i + 2, last)):
                send_ctx(j)

        @pl.when(upper)
        def _():
            pl.loop(finished(i), finished(i + 1))(finish)

        @pl.when(jnp.logical_not(upper))
        def _():
            finish(i)

    @pl.when(upper)
    def _():
        pl.loop(finished(blocks), blocks)(finish)


    @pl.when(h == 1)
    def _():
        own_grad.start()

    @pl.loop(0, blocks)
    def _(i):
        other_copy(i).wait_send()

        @pl.when(z > 0)
        def _():
            for part in range(ROW_PARTS):
                chain_copy(i, part).wait_send()

        pair_copy(i, d).wait()

        @pl.when(remote(i))
        def _():
            same_copy(i, owner(i, True)).wait()

    @pl.loop(0, last)
    def _(j):
        w_copy(j).wait()

        @pl.when(j != PARTNER_TURN)
        def _():
            ctx_copy(j).wait()

    own_ctx.wait()
    own_w.wait()
    own_pass.wait()

    @pl.when(h == 1)
    def _():
        own_grad.wait()


def suffix_and_columns(back, top, ctx, token_batch, plan, sections, owners):
    rows, width = ctx.shape
    dma = pltpu.SemaphoreType.DMA
    blocks = owners // 2
    return pl.pallas_call(
        functools.partial(suffix_kernel, sections, owners),
        out_shape=jax.ShapeDtypeStruct((3, owners, rows + W_ROWS, BLK), jnp.bfloat16),
        in_specs=[pl.BlockSpec(memory_space=pltpu.HBM)] * 3 + [
            pl.BlockSpec(memory_space=pltpu.VMEM),
            pl.BlockSpec(memory_space=pltpu.SMEM),
        ],
        out_specs=pl.BlockSpec(memory_space=pl.ANY),
        scratch_shapes=[
            pltpu.VMEM((rows, width), jnp.bfloat16),
            pltpu.VMEM((rows, width), jnp.bfloat16),
            pltpu.VMEM((W_ROWS, rows), jnp.bfloat16),
            pltpu.VMEM((5, blocks, rows, BLK), jnp.bfloat16),
        ] + [dma((blocks,))] * 2 + [dma((blocks * ROW_PARTS,))] * 2 + [dma((blocks,))] * 4
        + [dma((owners,))] * 4 + [dma((6,))],
        compiler_params=pltpu.CompilerParams(
            collective_id=0, has_side_effects=True, vmem_limit_bytes=54 * MIB),
        cost_estimate=pl.CostEstimate(flops=10 ** 7, bytes_accessed=10 ** 7, transcendentals=0),
    )(back, top, ctx, token_batch.reshape(1, rows), plan)


def split(x):
    high = x.astype(jnp.bfloat16)
    return high, (x - high.astype(jnp.float32)).astype(jnp.bfloat16)


def mm(a, b):
    return jnp.dot(a, b, preferred_element_type=jnp.float32)


PIECES = 4


def eye_block():
    rows = lax.broadcasted_iota(jnp.int32, (BLK, BLK), 0)
    return (rows == lax.broadcasted_iota(jnp.int32, (BLK, BLK), 1)).astype(jnp.float32)


def spectrum(squared):
    sums = jnp.sum(jnp.abs(squared), axis=0, keepdims=True)
    return jnp.sqrt(jnp.max(sums, axis=1, keepdims=True)) * 1.001


def first_steps(a, squared):
    top = spectrum(squared)
    reach = (top - damping) / (top + damping)
    scale = 2.0 / (top + damping)
    grow = 2.0 / (2.0 - reach * reach)
    eye = eye_block()
    inv = grow * (2.0 * scale * eye - (scale * scale) * a)
    residual = eye - grow * (2.0 * scale * a - (scale * scale) * squared)
    return inv, residual, after(reach)


def after(reach):
    return reach * reach / (2.0 - reach * reach)


def exact(a, b):
    return jnp.dot(a, b, precision=lax.Precision.HIGHEST, preferred_element_type=jnp.float32)


def inverse_kernel(
    tokens, owned, pre_ref,
    parts_ref, w_ref, weighted, mat, inv, mat_left, inv_left, inv_right, twice, sems,
):
    owners, tile, _ = parts_ref.shape
    eye = eye_block()
    piece = owners // PIECES
    loads = []
    for k in range(PIECES):
        some = pl.ds(k * piece, piece)
        loads.append((
            pltpu.make_async_copy(
                owned.at[0, some, pl.ds(0, tile)], parts_ref.at[some], sems.at[0, k]),
            pltpu.make_async_copy(
                owned.at[1, some, pl.ds(tile, W_ROWS), pl.ds(0, tile)], w_ref.at[some], sems.at[1, k]),
        ))
        for load in loads[-1]:
            load.start()

    def turn(t):
        at = pl.ds(t * tile, tile)
        w = w_ref[t, 0:1, :].astype(jnp.float32)
        weighted[:, at] = (parts_ref[t].astype(jnp.float32).T * w).astype(jnp.bfloat16)

    for k in range(PIECES):
        for load in loads[k]:
            load.wait()
        for t in range(k * piece, (k + 1) * piece):
            turn(t)

    def put_right(high, low):
        inv_right[0:BLK, :] = high
        inv_right[BLK:2 * BLK, :] = low
        inv_right[2 * BLK:3 * BLK, :] = high

    def put_inverse(x):
        inv[...] = x
        high, low = split(x)
        put_right(high, low)
        inv_left[:, 0:BLK] = high
        inv_left[:, BLK:2 * BLK] = low

    def put_residual(residual):
        residual = residual.astype(jnp.bfloat16)
        twice[0:BLK, :] = residual
        twice[BLK:2 * BLK, :] = residual

    grad = parts_ref[...].reshape(tokens, BLK)
    a = mm(weighted[...], grad) * (1.0 / tokens) + damping * eye
    mat[...] = a
    high, low = split(a)
    mat_left[:, 0:BLK] = high
    mat_left[:, BLK:2 * BLK] = high
    mat_left[:, 2 * BLK:3 * BLK] = low
    put_right(high, low)
    squared = mm(mat_left[...], inv_right[...])
    x, residual, reach = first_steps(a, squared)
    put_inverse(x)
    put_residual(residual)
    reach = jnp.max(reach)
    quick = jnp.max(spectrum(squared)) <= 512.0 * damping

    def quick_update(reach):
        step = mm(inv_left[...], twice[...])
        put_inverse((2.0 / (2.0 - reach * reach)) * (inv[...] + step))
        return after(reach)

    def quick_body(reach):
        put_residual(eye - mm(mat_left[...], inv_right[...]))
        return quick_update(reach)

    def full_body(reach):
        x = inv[...]
        inv[...] = (2.0 / (2.0 - reach * reach)) * (x + exact(x, eye - exact(mat[...], x)))
        return after(reach)

    @pl.when(quick)
    def _():
        lax.while_loop(lambda r: r > 1e-4, quick_body, quick_update(reach))

    @pl.when(jnp.logical_not(quick))
    def _():
        lax.while_loop(lambda r: r > 1e-6, full_body, reach)

    pre_ref[...] = mm(parts_ref[...].reshape(tokens, BLK), inv[...].astype(jnp.bfloat16)).astype(jnp.bfloat16)


def inverses(owned):
    _, owners, tile, _ = owned.shape
    tile = tile - W_ROWS
    tokens = owners * tile
    square = (BLK, BLK)
    return pl.pallas_call(
        functools.partial(inverse_kernel, tokens),
        out_shape=jax.ShapeDtypeStruct((tokens, BLK), jnp.bfloat16),
        in_specs=[pl.BlockSpec(memory_space=pl.ANY)],
        out_specs=pl.BlockSpec(memory_space=pltpu.VMEM),
        scratch_shapes=[
            pltpu.VMEM((owners, tile, BLK), jnp.bfloat16),
            pltpu.VMEM((owners, W_ROWS, tile), jnp.bfloat16),
            pltpu.VMEM((BLK, tokens), jnp.bfloat16),
            pltpu.VMEM(square, jnp.float32),
            pltpu.VMEM(square, jnp.float32),
            pltpu.VMEM((BLK, 3 * BLK), jnp.bfloat16),
            pltpu.VMEM((BLK, 2 * BLK), jnp.bfloat16),
            pltpu.VMEM((3 * BLK, BLK), jnp.bfloat16),
            pltpu.VMEM((2 * BLK, BLK), jnp.bfloat16),
            pltpu.SemaphoreType.DMA((2, PIECES)),
        ],
        compiler_params=pltpu.CompilerParams(vmem_limit_bytes=48 * MIB),
        cost_estimate=pl.CostEstimate(flops=2 * 10 ** 10, bytes_accessed=10 ** 7, transcendentals=0),
    )(owned)


DX = (0, 1, 3, 0, 2, 1, 3, 2)
DY = (0, 0, 0, 1, 0, 1, 1, 1)
CODE_X = sum(v << (2 * p) for p, v in enumerate(DX))
CODE_Y = sum(v << p for p, v in enumerate(DY))


def newton_steps(largest, goal):
    reach, steps = (largest - damping) / (largest + damping), 0
    while reach > goal:
        reach, steps = reach * reach / (2.0 - reach * reach), steps + 1
    return steps


INPUT_STEPS = newton_steps((BLK * 36.0 + damping) * 1.01, 1e-4)


def gather_kernel(
    owners, tokens,
    pre_ref, owned, out_ref,
    held, done, begun, ctx_ref, w_ref, ctx_t, pt_ref, mat, inv,
    send_up, send_down, send_y, send_sib, recv, recv_sib, own_sem, out_sem,
):
    d = lax.axis_index("dp")
    half = tokens // 2
    low, high = (0, half), (half, half)
    quarters = [(k * half // 2, half // 2) for k in range(4)]

    def place(p, dc):
        if isinstance(p, int):
            return neighbour(d, DY[p], DX[p], dc)
        dx = lax.shift_right_logical(jnp.int32(CODE_X), 2 * p) & 3
        dy = lax.shift_right_logical(jnp.int32(CODE_Y), p) & 1
        return neighbour(d, dy, dx, dc)

    up, down = neighbour(d, 0, 1, 0), neighbour(d, 0, 3, 0)
    across, sibling = neighbour(d, 1, 0, 0), neighbour(d, 0, 0, 1)

    barrier = pltpu.get_barrier_semaphore()
    for other in (up, down, across, sibling):
        pl.semaphore_signal(barrier, inc=1, device_id={"dp": other}, device_id_type=MESH)
    own = pltpu.make_async_copy(pre_ref, held.at[d], own_sem.at[0])
    own.start()
    tile = ctx_ref.shape[1]
    side = owners // 2
    here = pl.ds(pl.multiple_of(d // side * side, side), side)
    loads = [
        pltpu.make_async_copy(owned.at[1, here, pl.ds(0, tile)], ctx_ref.at[here], own_sem.at[1]),
        pltpu.make_async_copy(owned.at[1, :, pl.ds(tile, W_ROWS), pl.ds(0, tile)], w_ref, own_sem.at[2]),
    ]
    ctx_over = pltpu.make_async_remote_copy(
        src_ref=owned.at[2, here, pl.ds(0, tile)], dst_ref=ctx_ref.at[here],
        send_sem=own_sem.at[3], recv_sem=own_sem.at[4],
        device_id={"dp": across}, device_id_type=MESH)
    for load in loads:
        load.start()
    pl.semaphore_wait(barrier, 4)
    ctx_over.start()

    started = []
    slot = {low: 0, high: 2}
    slot.update((rows, k) for k, rows in enumerate(quarters))
    count = {"up": 0, "down": 0, "across": 0}

    def send(p, part, to, send_sem, recv_sem):
        rows = pl.ds(*part)
        target = held.at[place(p, 0), rows]
        copy = pltpu.make_async_remote_copy(
            src_ref=pre_ref.at[rows] if p == 0 else target, dst_ref=target,
            send_sem=send_sem, recv_sem=recv_sem,
            device_id={"dp": to}, device_id_type=MESH)
        copy.start()
        started.append(copy)

    def pass_on(way, p, part, there):
        to, sems = {"up": (up, send_up), "down": (down, send_down), "across": (across, send_y)}[way]
        send(p, part, to, sems.at[count[way]], recv.at[there, slot[part]])
        count[way] += 1

    def to_sibling(p, part):
        send(p, part, sibling, send_sib.at[p, slot[part]], recv_sib.at[p, slot[part]])

    def arrived(p, part, dc=0):
        at = held.at[place(p, dc), pl.ds(*part)]
        sems = recv_sib if dc else recv
        pltpu.make_async_copy(at, at, sems.at[p, slot[part]]).wait()

    def got(p, part):
        arrived(p, part)
        to_sibling(p, part)

    def out_copy(block):
        return pltpu.make_async_copy(done.at[block], out_ref.at[:, columns(block)], out_sem.at[block])

    def finish(block, total):
        done[block] = total.astype(jnp.bfloat16)
        out_copy(block).start()

    def multiply(p, dc):
        block = place(p, dc)
        finish(block, mm(pt_ref[...], held[block]))

    def partial(p, dc, *spans):
        block = place(p, dc)
        return sum(mm(pt_ref[:, a:b], held[block, a:b, :]) for a, b in spans)

    def begin_multiply(p, dc, *spans):
        begun[2 * (p - 5) + dc] = partial(p, dc, *spans)

    def go_on(p, dc, *spans):
        begun[2 * (p - 5) + dc] += partial(p, dc, *spans)

    def end_multiply(p, dc, *spans):
        finish(place(p, dc), begun[2 * (p - 5) + dc] + partial(p, dc, *spans))

    for k in range(2):
        pass_on("up", 0, quarters[k], 2)
        pass_on("down", 0, quarters[2 + k], 1)
    pass_on("across", 0, low, 3)
    pass_on("across", 0, high, 3)
    to_sibling(0, low)
    to_sibling(0, high)
    own.wait()
    for load in loads:
        load.wait()

    arrived(2, quarters[0])
    pass_on("up", 2, quarters[0], 4)
    arrived(1, quarters[2])
    pass_on("down", 1, quarters[2], 4)
    arrived(2, quarters[1])
    pass_on("up", 2, quarters[1], 4)
    pass_on("up", 0, high, 2)
    arrived(1, quarters[3])
    pass_on("down", 1, quarters[3], 4)
    pass_on("down", 0, low, 1)
    for k in range(2):
        to_sibling(2, quarters[k])
        to_sibling(1, quarters[2 + k])
    ctx_over.wait()

    @pl.loop(0, owners)
    def _(t):
        at = pl.ds(pl.multiple_of(t * tile, tile), tile)
        turned = ctx_ref[t].astype(jnp.float32).T
        ctx_t[:, at] = turned.astype(jnp.bfloat16)
        pt_ref[:, at] = (turned * w_ref[t, 0:1, :].astype(jnp.float32)).astype(jnp.bfloat16)

    eye = eye_block()
    mat[...] = mm(pt_ref[...], ctx_ref[...].reshape(tokens, BLK)) * (1.0 / tokens) + damping * eye
    x, residual, reach = first_steps(mat[...], exact(mat[...], mat[...]))
    inv[...] = (2.0 / (2.0 - reach * reach)) * (x + exact(x, residual))

    def newton(_, reach):
        x = inv[...]
        inv[...] = (2.0 / (2.0 - reach * reach)) * (x + exact(x, eye - exact(mat[...], x)))
        return after(reach)

    reach = lax.fori_loop(2, 4, newton, after(reach))
    for k in range(2):
        arrived(4, quarters[k])
        pass_on("across", 4, quarters[k], 7)
        arrived(4, quarters[2 + k])
        pass_on("across", 4, quarters[2 + k], 7)
    arrived(3, low)
    pass_on("up", 3, low, 6)
    pass_on("down", 3, low, 5)
    to_sibling(3, low)
    for k in range(4):
        to_sibling(4, quarters[k])

    reach = lax.fori_loop(4, 8, newton, reach)
    arrived(3, high)
    for k in range(2, 4):
        pass_on("up", 3, quarters[k], 6)
        pass_on("down", 3, quarters[k], 5)
    to_sibling(3, high)

    lax.fori_loop(8, INPUT_STEPS, newton, reach)
    ahead, behind = split(inv[...])
    rest_of_it = (inv[...] - ahead.astype(jnp.float32) - behind.astype(jnp.float32)).astype(jnp.bfloat16)
    pt_ref[...] = (
        mm(ahead, ctx_t[...]) + (mm(behind, ctx_t[...]) + mm(rest_of_it, ctx_t[...]))).astype(jnp.bfloat16)

    @pl.loop(0, 1)
    def _(p):
        multiply(p, 0)

    @pl.loop(3, 5)
    def _(p):
        multiply(p, 0)

    got(2, high)
    got(1, low)

    @pl.loop(1, 3)
    def _(p):
        multiply(p, 0)

    for rows in (low, high):
        arrived(0, rows, 1)
        arrived(3, rows, 1)
    for k in range(2):
        arrived(1, quarters[2 + k], 1)
        arrived(2, quarters[k], 1)
    for k in range(4):
        arrived(4, quarters[k], 1)
    arrived(1, low, 1)
    arrived(2, high, 1)

    @pl.loop(0, 5)
    def _(p):
        multiply(p, 1)

    got(5, low)
    got(6, low)
    got(7, quarters[0])
    got(7, quarters[2])
    soon = (0, half // 2), (half, half + half // 2)
    late = (half // 2, half), (half + half // 2, tokens)
    for dc in range(2):
        if dc:
            arrived(5, low, 1)
            arrived(6, low, 1)
            arrived(7, quarters[0], 1)
            arrived(7, quarters[2], 1)
        begin_multiply(5, dc, (0, half))
        begin_multiply(6, dc, (0, half))
        begin_multiply(7, dc, *soon)

    got(5, quarters[2])
    got(6, quarters[2])
    for dc in range(2):
        for p in (5, 6):
            if dc:
                arrived(p, quarters[2], 1)
            go_on(p, dc, (half, half + half // 2))

    got(7, quarters[1])
    got(7, quarters[3])
    got(5, quarters[3])
    got(6, quarters[3])
    for dc in range(2):
        if dc:
            arrived(7, quarters[1], 1)
            arrived(7, quarters[3], 1)
            arrived(5, quarters[3], 1)
            arrived(6, quarters[3], 1)
        end_multiply(7, dc, *late)
        end_multiply(5, dc, (half + half // 2, tokens))
        end_multiply(6, dc, (half + half // 2, tokens))

    for copy in started:
        copy.wait_send()

    @pl.loop(0, owners)
    def _(block):
        out_copy(block).wait()


def gather_and_multiply(pre, owned):
    tokens = pre.shape[0]
    _, owners, tile, _ = owned.shape
    tile = tile - W_ROWS
    dma = pltpu.SemaphoreType.DMA
    product = pl.pallas_call(
        functools.partial(gather_kernel, owners, tokens),
        out_shape=jax.ShapeDtypeStruct((BLK, owners * BLK), jnp.bfloat16),
        in_specs=[pl.BlockSpec(memory_space=pl.ANY)] * 2,
        out_specs=pl.BlockSpec(memory_space=pl.ANY),
        scratch_shapes=[
            pltpu.VMEM((owners, tokens, BLK), jnp.bfloat16),
            pltpu.VMEM((owners, BLK, BLK), jnp.bfloat16),
            pltpu.VMEM((6, BLK, BLK), jnp.float32),
            pltpu.VMEM((owners, tile, BLK), jnp.bfloat16),
            pltpu.VMEM((owners, W_ROWS, tile), jnp.bfloat16),
            pltpu.VMEM((BLK, tokens), jnp.bfloat16),
            pltpu.VMEM((BLK, tokens), jnp.bfloat16),
            pltpu.VMEM((BLK, BLK), jnp.float32),
            pltpu.VMEM((BLK, BLK), jnp.float32),
            dma((8,)), dma((8,)), dma((6,)), dma((8, 4)), dma((8, 4)), dma((8, 4)), dma((5,)), dma((owners,)),
        ],
        compiler_params=pltpu.CompilerParams(
            collective_id=1, has_side_effects=True, vmem_limit_bytes=46 * MIB),
        cost_estimate=pl.CostEstimate(flops=10 ** 10, bytes_accessed=10 ** 7, transcendentals=0),
    )(pre, owned)
    return product * jnp.bfloat16(1.0 / tokens)


def local(context, back_terms, top_grad, token_batch, plan):
    sections, owners = lax.axis_size("section"), lax.axis_size("dp")
    owned = suffix_and_columns(
        back_terms[0], top_grad, context[0], token_batch, plan, sections, owners)
    return gather_and_multiply(inverses(owned), owned)[None]


def solution(mesh):
    return jax.shard_map(
        local,
        mesh=mesh,
        in_specs=(P("section", "dp", None), P("section", "dp", None), P("dp", None), P("dp"), P()),
        out_specs=P("section", "dp", None),
        check_vma=False,
    )
```

```python
import functools

import jax
import jax.numpy as jnp
from jax import lax
from jax.experimental import pallas as pl
from jax.experimental.pallas import tpu as pltpu
from jax.sharding import PartitionSpec as P

BLK = 384
MB = 8
MESH = pl.DeviceIdType.MESH
MIB = 1 << 20

falloff = 0.5
damping = 0.1


def columns(block):
    return pl.ds(pl.multiple_of(block * BLK, BLK), BLK)


ROW_PARTS = 8
W_ROWS = 16

OTHER, SUM, NEXT, GRAD = 0, 1, 2, 3

ORDER_X = (1, 3, 2, 0, 3, 1, 2, 0)
ORDER_Y = (0, 1, 0, 1, 0, 1, 1, 0)
CODE_ORDER_X = sum(v << (2 * p) for p, v in enumerate(ORDER_X))
CODE_ORDER_Y = sum(v << p for p, v in enumerate(ORDER_Y))


def neighbour(d, dy, dx, dc):
    y, x, c = d // 8, lax.rem(d // 2, 4), lax.rem(d, 2)
    return lax.rem(y + dy, 2) * 8 + lax.rem(x + dx, 4) * 2 + lax.rem(c + dc, 2)


def in_turn(d, j):
    q = lax.rem(j, 8)
    dx = lax.shift_right_logical(jnp.int32(CODE_ORDER_X), 2 * q) & 3
    dy = lax.shift_right_logical(jnp.int32(CODE_ORDER_Y), q) & 1
    return neighbour(d, dy, dx, 1 - j // 8)


PARTNER_TURN = 8 + next(q for q in range(8) if (ORDER_X[q], ORDER_Y[q]) == (0, 1))


def over_y(j):
    return lax.shift_right_logical(jnp.int32(CODE_ORDER_Y), lax.rem(j, 8)) & 1


def suffix_kernel(
    sections, owners,
    back_hbm, top_hbm, ctx_ref, batch_ref, plan_ref,
    owned,
    back_ref, top_ref, w_ref, bufs,
    other_send, other_recv, chain_send, chain_recv, pair_send, pair_recv, same_send, same_recv,
    ctx_send, ctx_recv, w_send, w_recv, own_sem,
):
    s = lax.axis_index("section")
    d = lax.axis_index("dp")
    z, h = s // 2, s % 2
    levels = sections // 2
    below = lax.rem(s + sections - 2, sections)
    above = lax.rem(s + 2, sections)
    pair = s + 1 - 2 * h
    size = back_ref.shape[0] // ROW_PARTS
    blocks = owners // 2
    last = owners - 1

    loads = [
        pltpu.make_async_copy(back_hbm, back_ref, own_sem.at[0]),
        pltpu.make_async_copy(top_hbm, top_ref, own_sem.at[1]),
    ]
    for load in loads:
        load.start()

    barrier = pltpu.get_barrier_semaphore()
    for other in (below, above):
        pl.semaphore_signal(barrier, inc=1, device_id={"section": other}, device_id_type=MESH)

    @pl.loop(0, owners)
    def _(j):
        pl.semaphore_signal(barrier, inc=1, device_id={"section": pair, "dp": j}, device_id_type=MESH)

        @pl.when(j > 0)
        def _():
            pl.semaphore_signal(barrier, inc=1, device_id={"dp": lax.rem(d + j, owners)}, device_id_type=MESH)

    weight = jnp.zeros(batch_ref.shape, jnp.float32)
    for slot in range(MB):
        late = MB - 1 - plan_ref[slot]
        value = jnp.float32(1.0)
        for bit in range(3):
            value = value * jnp.where((late & (1 << bit)) != 0, jnp.float32(falloff ** (1 << bit)), jnp.float32(1.0))
        weight = jnp.where(batch_ref[...] == slot, value, weight)
    w_ref[...] = jnp.broadcast_to(weight, w_ref.shape).astype(w_ref.dtype)

    @pl.when(z == levels - 1)
    def _():
        @pl.loop(0, blocks)
        def _(j):
            bufs[SUM, j] = jnp.zeros(bufs.shape[2:], bufs.dtype)

    pl.semaphore_wait(barrier, 2 * owners + 1)

    every_row = pl.ds(0, back_ref.shape[0])
    rows_of_grad = owned.at[0, d, every_row]
    rows_of_ctx = owned.at[1, d, every_row]
    rows_to_pass = owned.at[2, d, every_row]
    rows_of_w = owned.at[1, d, pl.ds(back_ref.shape[0], w_ref.shape[0]), pl.ds(0, w_ref.shape[1])]

    across = neighbour(d, 1, 0, 0)

    def ctx_copy(j):
        to, dy = in_turn(d, j), over_y(j)
        return pltpu.make_async_remote_copy(
            src_ref=ctx_ref.at[:, columns(to)], dst_ref=owned.at[1 + dy, d, every_row],
            send_sem=ctx_send.at[j], recv_sem=ctx_recv.at[j],
            device_id={"dp": neighbour(to, dy, 0, 0)}, device_id_type=MESH)

    def w_copy(j):
        to = in_turn(d, j)
        return pltpu.make_async_remote_copy(
            src_ref=w_ref, dst_ref=rows_of_w,
            send_sem=w_send.at[j], recv_sem=w_recv.at[j],
            device_id={"dp": to}, device_id_type=MESH)

    def owner(i, mine):
        return in_turn(d, i + blocks * jnp.where(mine, h, 1 - h))

    def other_copy(i):
        return pltpu.make_async_remote_copy(
            src_ref=back_hbm.at[:, columns(owner(i, False))], dst_ref=bufs.at[OTHER, i],
            send_sem=other_send.at[i], recv_sem=other_recv.at[i],
            device_id={"section": pair}, device_id_type=MESH)

    def chain_copy(i, part):
        k, rows = i * ROW_PARTS + part, pl.ds(part * size, size)
        return pltpu.make_async_remote_copy(
            src_ref=bufs.at[NEXT, i, rows], dst_ref=bufs.at[SUM, i, rows],
            send_sem=chain_send.at[k], recv_sem=chain_recv.at[k],
            device_id={"section": below}, device_id_type=MESH)

    def pair_copy(i, to):
        return pltpu.make_async_remote_copy(
            src_ref=bufs.at[GRAD + 1 - h, i], dst_ref=rows_of_grad,
            send_sem=pair_send.at[i], recv_sem=pair_recv.at[i],
            device_id={"section": pair, "dp": to}, device_id_type=MESH)

    def same_copy(i, to):
        return pltpu.make_async_remote_copy(
            src_ref=bufs.at[GRAD + h, i], dst_ref=rows_of_grad,
            send_sem=same_send.at[i], recv_sem=same_recv.at[i],
            device_id={"dp": to}, device_id_type=MESH)

    def remote(i):
        return (h == 0) | (i < blocks - 1)

    own_ctx = pltpu.make_async_copy(ctx_ref.at[:, columns(d)], rows_of_ctx, own_sem.at[2])
    own_w = pltpu.make_async_copy(w_ref, rows_of_w, own_sem.at[3])
    own_grad = pltpu.make_async_copy(bufs.at[GRAD + 1, blocks - 1], rows_of_grad, own_sem.at[4])

    @pl.loop(0, blocks)
    def _(i):
        other_copy(i).start()

    own_pass = pltpu.make_async_copy(ctx_ref.at[:, columns(across)], rows_to_pass, own_sem.at[5])
    own_ctx.start()
    own_w.start()
    own_pass.start()

    def send_ctx(j):
        w_copy(j).start()

        @pl.when(j != PARTNER_TURN)
        def _():
            ctx_copy(j).start()

    head = z == levels - 1

    @pl.when(jnp.logical_not(head))
    def _():
        pl.loop(0, last)(send_ctx)

    for load in loads:
        load.wait()

    later = jnp.where(z < levels // 2, -blocks, z - 1)

    def finished(i):
        return jnp.clip(2 * (i - later), 0, i)

    def finish(i):
        to = owner(i, True)
        cols = columns(to)
        odd = bufs[SUM, i].astype(jnp.float32) + top_ref[:, cols].astype(jnp.float32)
        bufs[GRAD + 1, i] = odd.astype(jnp.bfloat16)

        @pl.when(h == 0)
        def _():
            bufs[GRAD, i] = (odd + bufs[OTHER, i].astype(jnp.float32)).astype(jnp.bfloat16)

        @pl.when(h == 1)
        def _():
            bufs[GRAD, i] = (odd + back_ref[:, cols].astype(jnp.float32)).astype(jnp.bfloat16)

        pair_copy(i, to).start()

        @pl.when(remote(i))
        def _():
            same_copy(i, to).start()

    @pl.loop(0, blocks)
    def _(i):
        cols = columns(owner(i, True))
        other_copy(i).wait_recv()
        for part in range(ROW_PARTS):
            rows = pl.ds(part * size, size)

            @pl.when(z < levels - 1)
            def _():
                chain_copy(i, part).wait_recv()

            @pl.when(z > 0)
            def _():
                here = back_ref[rows, cols].astype(jnp.float32) + bufs[OTHER, i, rows, :].astype(jnp.float32)
                bufs[NEXT, i, rows, :] = (bufs[SUM, i, rows, :].astype(jnp.float32) + here).astype(jnp.bfloat16)
                chain_copy(i, part).start()

        @pl.when(head)
        def _():
            send_ctx(2 * i)

            @pl.when(i < blocks - 1)
            def _():
                send_ctx(2 * i + 1)

        pl.loop(finished(i), finished(i + 1))(finish)

    pl.loop(finished(blocks), blocks)(finish)

    @pl.when(h == 1)
    def _():
        own_grad.start()

    @pl.loop(0, blocks)
    def _(i):
        other_copy(i).wait_send()

        @pl.when(z > 0)
        def _():
            for part in range(ROW_PARTS):
                chain_copy(i, part).wait_send()

        pair_copy(i, d).wait()

        @pl.when(remote(i))
        def _():
            same_copy(i, owner(i, True)).wait()

    @pl.loop(0, last)
    def _(j):
        w_copy(j).wait()

        @pl.when(j != PARTNER_TURN)
        def _():
            ctx_copy(j).wait()

    own_ctx.wait()
    own_w.wait()
    own_pass.wait()

    @pl.when(h == 1)
    def _():
        own_grad.wait()


def suffix_and_columns(back, top, ctx, token_batch, plan, sections, owners):
    rows, width = ctx.shape
    dma = pltpu.SemaphoreType.DMA
    blocks = owners // 2
    return pl.pallas_call(
        functools.partial(suffix_kernel, sections, owners),
        out_shape=jax.ShapeDtypeStruct((3, owners, rows + W_ROWS, BLK), jnp.bfloat16),
        in_specs=[pl.BlockSpec(memory_space=pltpu.HBM)] * 3 + [
            pl.BlockSpec(memory_space=pltpu.VMEM),
            pl.BlockSpec(memory_space=pltpu.SMEM),
        ],
        out_specs=pl.BlockSpec(memory_space=pl.ANY),
        scratch_shapes=[
            pltpu.VMEM((rows, width), jnp.bfloat16),
            pltpu.VMEM((rows, width), jnp.bfloat16),
            pltpu.VMEM((W_ROWS, rows), jnp.bfloat16),
            pltpu.VMEM((5, blocks, rows, BLK), jnp.bfloat16),
        ] + [dma((blocks,))] * 2 + [dma((blocks * ROW_PARTS,))] * 2 + [dma((blocks,))] * 4
        + [dma((owners,))] * 4 + [dma((6,))],
        compiler_params=pltpu.CompilerParams(
            collective_id=0, has_side_effects=True, vmem_limit_bytes=54 * MIB),
        cost_estimate=pl.CostEstimate(flops=10 ** 7, bytes_accessed=10 ** 7, transcendentals=0),
    )(back, top, ctx, token_batch.reshape(1, rows), plan)


def split(x):
    high = x.astype(jnp.bfloat16)
    return high, (x - high.astype(jnp.float32)).astype(jnp.bfloat16)


def mm(a, b):
    return jnp.dot(a, b, preferred_element_type=jnp.float32)


PIECES = 4


def eye_block():
    rows = lax.broadcasted_iota(jnp.int32, (BLK, BLK), 0)
    return (rows == lax.broadcasted_iota(jnp.int32, (BLK, BLK), 1)).astype(jnp.float32)


def spectrum(squared):
    sums = jnp.sum(jnp.abs(squared), axis=0, keepdims=True)
    return jnp.sqrt(jnp.max(sums, axis=1, keepdims=True)) * 1.001


def first_steps(a, squared):
    top = spectrum(squared)
    reach = (top - damping) / (top + damping)
    scale = 2.0 / (top + damping)
    grow = 2.0 / (2.0 - reach * reach)
    eye = eye_block()
    inv = grow * (2.0 * scale * eye - (scale * scale) * a)
    residual = eye - grow * (2.0 * scale * a - (scale * scale) * squared)
    return inv, residual, after(reach)


def after(reach):
    return reach * reach / (2.0 - reach * reach)


def exact(a, b):
    return jnp.dot(a, b, precision=lax.Precision.HIGHEST, preferred_element_type=jnp.float32)


def inverse_kernel(
    tokens, owned, pre_ref,
    parts_ref, w_ref, weighted, mat, inv, mat_left, inv_left, inv_right, twice, sems,
):
    owners, tile, _ = parts_ref.shape
    eye = eye_block()
    piece = owners // PIECES
    loads = []
    for k in range(PIECES):
        some = pl.ds(k * piece, piece)
        loads.append((
            pltpu.make_async_copy(
                owned.at[0, some, pl.ds(0, tile)], parts_ref.at[some], sems.at[0, k]),
            pltpu.make_async_copy(
                owned.at[1, some, pl.ds(tile, W_ROWS), pl.ds(0, tile)], w_ref.at[some], sems.at[1, k]),
        ))
        for load in loads[-1]:
            load.start()

    def turn(t):
        at = pl.ds(t * tile, tile)
        w = w_ref[t, 0:1, :].astype(jnp.float32)
        weighted[:, at] = (parts_ref[t].astype(jnp.float32).T * w).astype(jnp.bfloat16)

    for k in range(PIECES):
        for load in loads[k]:
            load.wait()
        for t in range(k * piece, (k + 1) * piece):
            turn(t)

    def put_right(high, low):
        inv_right[0:BLK, :] = high
        inv_right[BLK:2 * BLK, :] = low
        inv_right[2 * BLK:3 * BLK, :] = high

    def put_inverse(x):
        inv[...] = x
        high, low = split(x)
        put_right(high, low)
        inv_left[:, 0:BLK] = high
        inv_left[:, BLK:2 * BLK] = low

    def put_residual(residual):
        residual = residual.astype(jnp.bfloat16)
        twice[0:BLK, :] = residual
        twice[BLK:2 * BLK, :] = residual

    grad = parts_ref[...].reshape(tokens, BLK)
    a = mm(weighted[...], grad) * (1.0 / tokens) + damping * eye
    mat[...] = a
    high, low = split(a)
    mat_left[:, 0:BLK] = high
    mat_left[:, BLK:2 * BLK] = high
    mat_left[:, 2 * BLK:3 * BLK] = low
    put_right(high, low)
    squared = mm(mat_left[...], inv_right[...])
    x, residual, reach = first_steps(a, squared)
    put_inverse(x)
    put_residual(residual)
    reach = jnp.max(reach)
    quick = jnp.max(spectrum(squared)) <= 512.0 * damping

    def quick_update(reach):
        step = mm(inv_left[...], twice[...])
        put_inverse((2.0 / (2.0 - reach * reach)) * (inv[...] + step))
        return after(reach)

    def quick_body(reach):
        put_residual(eye - mm(mat_left[...], inv_right[...]))
        return quick_update(reach)

    def full_body(reach):
        x = inv[...]
        inv[...] = (2.0 / (2.0 - reach * reach)) * (x + exact(x, eye - exact(mat[...], x)))
        return after(reach)

    @pl.when(quick)
    def _():
        lax.while_loop(lambda r: r > 1e-4, quick_body, quick_update(reach))

    @pl.when(jnp.logical_not(quick))
    def _():
        lax.while_loop(lambda r: r > 1e-6, full_body, reach)

    pre_ref[...] = mm(parts_ref[...].reshape(tokens, BLK), inv[...].astype(jnp.bfloat16)).astype(jnp.bfloat16)


def inverses(owned):
    _, owners, tile, _ = owned.shape
    tile = tile - W_ROWS
    tokens = owners * tile
    square = (BLK, BLK)
    return pl.pallas_call(
        functools.partial(inverse_kernel, tokens),
        out_shape=jax.ShapeDtypeStruct((tokens, BLK), jnp.bfloat16),
        in_specs=[pl.BlockSpec(memory_space=pl.ANY)],
        out_specs=pl.BlockSpec(memory_space=pltpu.VMEM),
        scratch_shapes=[
            pltpu.VMEM((owners, tile, BLK), jnp.bfloat16),
            pltpu.VMEM((owners, W_ROWS, tile), jnp.bfloat16),
            pltpu.VMEM((BLK, tokens), jnp.bfloat16),
            pltpu.VMEM(square, jnp.float32),
            pltpu.VMEM(square, jnp.float32),
            pltpu.VMEM((BLK, 3 * BLK), jnp.bfloat16),
            pltpu.VMEM((BLK, 2 * BLK), jnp.bfloat16),
            pltpu.VMEM((3 * BLK, BLK), jnp.bfloat16),
            pltpu.VMEM((2 * BLK, BLK), jnp.bfloat16),
            pltpu.SemaphoreType.DMA((2, PIECES)),
        ],
        compiler_params=pltpu.CompilerParams(vmem_limit_bytes=48 * MIB),
        cost_estimate=pl.CostEstimate(flops=2 * 10 ** 10, bytes_accessed=10 ** 7, transcendentals=0),
    )(owned)


DX = (0, 1, 3, 0, 2, 1, 3, 2)
DY = (0, 0, 0, 1, 0, 1, 1, 1)
CODE_X = sum(v << (2 * p) for p, v in enumerate(DX))
CODE_Y = sum(v << p for p, v in enumerate(DY))


def newton_steps(largest, goal):
    reach, steps = (largest - damping) / (largest + damping), 0
    while reach > goal:
        reach, steps = reach * reach / (2.0 - reach * reach), steps + 1
    return steps


INPUT_STEPS = newton_steps((BLK * 36.0 + damping) * 1.01, 1e-4)


def gather_kernel(
    owners, tokens,
    pre_ref, owned, out_ref,
    held, done, begun, ctx_ref, w_ref, ctx_t, pt_ref, mat, inv,
    send_up, send_down, send_y, send_sib, recv, recv_sib, own_sem, out_sem,
):
    d = lax.axis_index("dp")
    half = tokens // 2
    low, high = (0, half), (half, half)
    quarters = [(k * half // 2, half // 2) for k in range(4)]

    def place(p, dc):
        if isinstance(p, int):
            return neighbour(d, DY[p], DX[p], dc)
        dx = lax.shift_right_logical(jnp.int32(CODE_X), 2 * p) & 3
        dy = lax.shift_right_logical(jnp.int32(CODE_Y), p) & 1
        return neighbour(d, dy, dx, dc)

    up, down = neighbour(d, 0, 1, 0), neighbour(d, 0, 3, 0)
    across, sibling = neighbour(d, 1, 0, 0), neighbour(d, 0, 0, 1)

    barrier = pltpu.get_barrier_semaphore()
    for other in (up, down, across, sibling):
        pl.semaphore_signal(barrier, inc=1, device_id={"dp": other}, device_id_type=MESH)
    own = pltpu.make_async_copy(pre_ref, held.at[d], own_sem.at[0])
    own.start()
    tile = ctx_ref.shape[1]
    side = owners // 2
    here = pl.ds(pl.multiple_of(d // side * side, side), side)
    loads = [
        pltpu.make_async_copy(owned.at[1, here, pl.ds(0, tile)], ctx_ref.at[here], own_sem.at[1]),
        pltpu.make_async_copy(owned.at[1, :, pl.ds(tile, W_ROWS), pl.ds(0, tile)], w_ref, own_sem.at[2]),
    ]
    ctx_over = pltpu.make_async_remote_copy(
        src_ref=owned.at[2, here, pl.ds(0, tile)], dst_ref=ctx_ref.at[here],
        send_sem=own_sem.at[3], recv_sem=own_sem.at[4],
        device_id={"dp": across}, device_id_type=MESH)
    for load in loads:
        load.start()
    pl.semaphore_wait(barrier, 4)
    ctx_over.start()

    started = []
    slot = {low: 0, high: 2}
    slot.update((rows, k) for k, rows in enumerate(quarters))
    count = {"up": 0, "down": 0, "across": 0}

    def send(p, part, to, send_sem, recv_sem):
        rows = pl.ds(*part)
        target = held.at[place(p, 0), rows]
        copy = pltpu.make_async_remote_copy(
            src_ref=pre_ref.at[rows] if p == 0 else target, dst_ref=target,
            send_sem=send_sem, recv_sem=recv_sem,
            device_id={"dp": to}, device_id_type=MESH)
        copy.start()
        started.append(copy)

    def pass_on(way, p, part, there):
        to, sems = {"up": (up, send_up), "down": (down, send_down), "across": (across, send_y)}[way]
        send(p, part, to, sems.at[count[way]], recv.at[there, slot[part]])
        count[way] += 1

    def to_sibling(p, part):
        send(p, part, sibling, send_sib.at[p, slot[part]], recv_sib.at[p, slot[part]])

    def arrived(p, part, dc=0):
        at = held.at[place(p, dc), pl.ds(*part)]
        sems = recv_sib if dc else recv
        pltpu.make_async_copy(at, at, sems.at[p, slot[part]]).wait()

    def got(p, part):
        arrived(p, part)
        to_sibling(p, part)

    def out_copy(block):
        return pltpu.make_async_copy(done.at[block], out_ref.at[:, columns(block)], out_sem.at[block])

    def finish(block, total):
        done[block] = total.astype(jnp.bfloat16)
        out_copy(block).start()

    def multiply(p, dc):
        block = place(p, dc)
        finish(block, mm(pt_ref[...], held[block]))

    def partial(p, dc, *spans):
        block = place(p, dc)
        return sum(mm(pt_ref[:, a:b], held[block, a:b, :]) for a, b in spans)

    def begin_multiply(p, dc, *spans):
        begun[2 * (p - 5) + dc] = partial(p, dc, *spans)

    def go_on(p, dc, *spans):
        begun[2 * (p - 5) + dc] += partial(p, dc, *spans)

    def end_multiply(p, dc, *spans):
        finish(place(p, dc), begun[2 * (p - 5) + dc] + partial(p, dc, *spans))

    for k in range(2):
        pass_on("up", 0, quarters[k], 2)
        pass_on("down", 0, quarters[2 + k], 1)
    pass_on("across", 0, low, 3)
    pass_on("across", 0, high, 3)
    to_sibling(0, low)
    to_sibling(0, high)
    own.wait()
    for load in loads:
        load.wait()

    arrived(2, quarters[0])
    pass_on("up", 2, quarters[0], 4)
    arrived(1, quarters[2])
    pass_on("down", 1, quarters[2], 4)
    arrived(2, quarters[1])
    pass_on("up", 2, quarters[1], 4)
    pass_on("up", 0, high, 2)
    arrived(1, quarters[3])
    pass_on("down", 1, quarters[3], 4)
    pass_on("down", 0, low, 1)
    for k in range(2):
        to_sibling(2, quarters[k])
        to_sibling(1, quarters[2 + k])
    ctx_over.wait()

    @pl.loop(0, owners)
    def _(t):
        at = pl.ds(pl.multiple_of(t * tile, tile), tile)
        turned = ctx_ref[t].astype(jnp.float32).T
        ctx_t[:, at] = turned.astype(jnp.bfloat16)
        pt_ref[:, at] = (turned * w_ref[t, 0:1, :].astype(jnp.float32)).astype(jnp.bfloat16)

    eye = eye_block()
    mat[...] = mm(pt_ref[...], ctx_ref[...].reshape(tokens, BLK)) * (1.0 / tokens) + damping * eye
    x, residual, reach = first_steps(mat[...], exact(mat[...], mat[...]))
    inv[...] = (2.0 / (2.0 - reach * reach)) * (x + exact(x, residual))

    def newton(_, reach):
        x = inv[...]
        inv[...] = (2.0 / (2.0 - reach * reach)) * (x + exact(x, eye - exact(mat[...], x)))
        return after(reach)

    reach = lax.fori_loop(2, 4, newton, after(reach))
    for k in range(2):
        arrived(4, quarters[k])
        pass_on("across", 4, quarters[k], 7)
        arrived(4, quarters[2 + k])
        pass_on("across", 4, quarters[2 + k], 7)
    arrived(3, low)
    pass_on("up", 3, low, 6)
    pass_on("down", 3, low, 5)
    to_sibling(3, low)
    for k in range(4):
        to_sibling(4, quarters[k])

    reach = lax.fori_loop(4, 8, newton, reach)
    arrived(3, high)
    for k in range(2, 4):
        pass_on("up", 3, quarters[k], 6)
        pass_on("down", 3, quarters[k], 5)
    to_sibling(3, high)

    lax.fori_loop(8, INPUT_STEPS, newton, reach)
    ahead, behind = split(inv[...])
    rest_of_it = (inv[...] - ahead.astype(jnp.float32) - behind.astype(jnp.float32)).astype(jnp.bfloat16)
    pt_ref[...] = (
        mm(ahead, ctx_t[...]) + (mm(behind, ctx_t[...]) + mm(rest_of_it, ctx_t[...]))).astype(jnp.bfloat16)

    @pl.loop(0, 1)
    def _(p):
        multiply(p, 0)

    @pl.loop(3, 5)
    def _(p):
        multiply(p, 0)

    got(2, high)
    got(1, low)

    @pl.loop(1, 3)
    def _(p):
        multiply(p, 0)

    for rows in (low, high):
        arrived(0, rows, 1)
        arrived(3, rows, 1)
    for k in range(2):
        arrived(1, quarters[2 + k], 1)
        arrived(2, quarters[k], 1)
    for k in range(4):
        arrived(4, quarters[k], 1)
    arrived(1, low, 1)
    arrived(2, high, 1)

    @pl.loop(0, 5)
    def _(p):
        multiply(p, 1)

    got(5, low)
    got(6, low)
    got(7, quarters[0])
    got(7, quarters[2])
    soon = (0, half // 2), (half, half + half // 2)
    late = (half // 2, half), (half + half // 2, tokens)
    for dc in range(2):
        if dc:
            arrived(5, low, 1)
            arrived(6, low, 1)
            arrived(7, quarters[0], 1)
            arrived(7, quarters[2], 1)
        begin_multiply(5, dc, (0, half))
        begin_multiply(6, dc, (0, half))
        begin_multiply(7, dc, *soon)

    got(5, quarters[2])
    got(6, quarters[2])
    for dc in range(2):
        for p in (5, 6):
            if dc:
                arrived(p, quarters[2], 1)
            go_on(p, dc, (half, half + half // 2))

    got(7, quarters[1])
    got(7, quarters[3])
    got(5, quarters[3])
    got(6, quarters[3])
    for dc in range(2):
        if dc:
            arrived(7, quarters[1], 1)
            arrived(7, quarters[3], 1)
            arrived(5, quarters[3], 1)
            arrived(6, quarters[3], 1)
        end_multiply(7, dc, *late)
        end_multiply(5, dc, (half + half // 2, tokens))
        end_multiply(6, dc, (half + half // 2, tokens))

    for copy in started:
        copy.wait_send()

    @pl.loop(0, owners)
    def _(block):
        out_copy(block).wait()


def gather_and_multiply(pre, owned):
    tokens = pre.shape[0]
    _, owners, tile, _ = owned.shape
    tile = tile - W_ROWS
    dma = pltpu.SemaphoreType.DMA
    product = pl.pallas_call(
        functools.partial(gather_kernel, owners, tokens),
        out_shape=jax.ShapeDtypeStruct((BLK, owners * BLK), jnp.bfloat16),
        in_specs=[pl.BlockSpec(memory_space=pl.ANY)] * 2,
        out_specs=pl.BlockSpec(memory_space=pl.ANY),
        scratch_shapes=[
            pltpu.VMEM((owners, tokens, BLK), jnp.bfloat16),
            pltpu.VMEM((owners, BLK, BLK), jnp.bfloat16),
            pltpu.VMEM((6, BLK, BLK), jnp.float32),
            pltpu.VMEM((owners, tile, BLK), jnp.bfloat16),
            pltpu.VMEM((owners, W_ROWS, tile), jnp.bfloat16),
            pltpu.VMEM((BLK, tokens), jnp.bfloat16),
            pltpu.VMEM((BLK, tokens), jnp.bfloat16),
            pltpu.VMEM((BLK, BLK), jnp.float32),
            pltpu.VMEM((BLK, BLK), jnp.float32),
            dma((8,)), dma((8,)), dma((6,)), dma((8, 4)), dma((8, 4)), dma((8, 4)), dma((5,)), dma((owners,)),
        ],
        compiler_params=pltpu.CompilerParams(
            collective_id=1, has_side_effects=True, vmem_limit_bytes=46 * MIB),
        cost_estimate=pl.CostEstimate(flops=10 ** 10, bytes_accessed=10 ** 7, transcendentals=0),
    )(pre, owned)
    return product * jnp.bfloat16(1.0 / tokens)


def local(context, back_terms, top_grad, token_batch, plan):
    sections, owners = lax.axis_size("section"), lax.axis_size("dp")
    owned = suffix_and_columns(
        back_terms[0], top_grad, context[0], token_batch, plan, sections, owners)
    return gather_and_multiply(inverses(owned), owned)[None]


def solution(mesh):
    return jax.shard_map(
        local,
        mesh=mesh,
        in_specs=(P("section", "dp", None), P("section", "dp", None), P("dp", None), P("dp"), P()),
        out_specs=P("section", "dp", None),
        check_vma=False,
    )
```

```python
import functools

import jax
import jax.numpy as jnp
from jax import lax
from jax.experimental import pallas as pl
from jax.experimental.pallas import tpu as pltpu
from jax.sharding import PartitionSpec as P

BLK = 384
MB = 8
MESH = pl.DeviceIdType.MESH
MIB = 1 << 20

falloff = 0.5
damping = 0.1


def columns(block):
    return pl.ds(pl.multiple_of(block * BLK, BLK), BLK)


ROW_PARTS = 4
W_ROWS = 16

OTHER, SUM, NEXT, GRAD = 0, 1, 2, 3

ORDER_X = (1, 3, 2, 0, 3, 1, 2, 0)
ORDER_Y = (0, 1, 0, 1, 0, 1, 1, 0)
CODE_ORDER_X = sum(v << (2 * p) for p, v in enumerate(ORDER_X))
CODE_ORDER_Y = sum(v << p for p, v in enumerate(ORDER_Y))


def neighbour(d, dy, dx, dc):
    y, x, c = d // 8, lax.rem(d // 2, 4), lax.rem(d, 2)
    return lax.rem(y + dy, 2) * 8 + lax.rem(x + dx, 4) * 2 + lax.rem(c + dc, 2)


def in_turn(d, j):
    q = lax.rem(j, 8)
    dx = lax.shift_right_logical(jnp.int32(CODE_ORDER_X), 2 * q) & 3
    dy = lax.shift_right_logical(jnp.int32(CODE_ORDER_Y), q) & 1
    return neighbour(d, dy, dx, 1 - j // 8)


PARTNER_TURN = 8 + next(q for q in range(8) if (ORDER_X[q], ORDER_Y[q]) == (0, 1))


def over_y(j):
    return lax.shift_right_logical(jnp.int32(CODE_ORDER_Y), lax.rem(j, 8)) & 1


def suffix_kernel(
    sections, owners,
    back_hbm, top_hbm, ctx_ref, batch_ref, plan_ref,
    owned,
    back_ref, top_ref, w_ref, bufs,
    other_send, other_recv, chain_send, chain_recv, pair_send, pair_recv, same_send, same_recv,
    ctx_send, ctx_recv, w_send, w_recv, own_sem,
):
    s = lax.axis_index("section")
    d = lax.axis_index("dp")
    z, h = s // 2, s % 2
    levels = sections // 2
    below = lax.rem(s + sections - 2, sections)
    above = lax.rem(s + 2, sections)
    pair = s + 1 - 2 * h
    size = back_ref.shape[0] // ROW_PARTS
    blocks = owners // 2
    last = owners - 1

    loads = [
        pltpu.make_async_copy(back_hbm, back_ref, own_sem.at[0]),
        pltpu.make_async_copy(top_hbm, top_ref, own_sem.at[1]),
    ]
    for load in loads:
        load.start()

    barrier = pltpu.get_barrier_semaphore()
    for other in (below, above):
        pl.semaphore_signal(barrier, inc=1, device_id={"section": other}, device_id_type=MESH)

    @pl.loop(0, owners)
    def _(j):
        pl.semaphore_signal(barrier, inc=1, device_id={"section": pair, "dp": j}, device_id_type=MESH)

        @pl.when(j > 0)
        def _():
            pl.semaphore_signal(barrier, inc=1, device_id={"dp": lax.rem(d + j, owners)}, device_id_type=MESH)

    weight = jnp.zeros(batch_ref.shape, jnp.float32)
    for slot in range(MB):
        late = MB - 1 - plan_ref[slot]
        value = jnp.float32(1.0)
        for bit in range(3):
            value = value * jnp.where((late & (1 << bit)) != 0, jnp.float32(falloff ** (1 << bit)), jnp.float32(1.0))
        weight = jnp.where(batch_ref[...] == slot, value, weight)
    w_ref[...] = jnp.broadcast_to(weight, w_ref.shape).astype(w_ref.dtype)

    @pl.when(z == levels - 1)
    def _():
        @pl.loop(0, blocks)
        def _(j):
            bufs[SUM, j] = jnp.zeros(bufs.shape[2:], bufs.dtype)

    pl.semaphore_wait(barrier, 2 * owners + 1)

    every_row = pl.ds(0, back_ref.shape[0])
    rows_of_grad = owned.at[0, d, every_row]
    rows_of_ctx = owned.at[1, d, every_row]
    rows_to_pass = owned.at[2, d, every_row]
    rows_of_w = owned.at[1, d, pl.ds(back_ref.shape[0], w_ref.shape[0]), pl.ds(0, w_ref.shape[1])]

    across = neighbour(d, 1, 0, 0)
    lower = z < levels // 2

    def ctx_copy(j):
        to, dy = in_turn(d, j), jnp.where(lower, 0, over_y(j))
        return pltpu.make_async_remote_copy(
            src_ref=ctx_ref.at[:, columns(to)], dst_ref=owned.at[1 + dy, d, every_row],
            send_sem=ctx_send.at[j], recv_sem=ctx_recv.at[j],
            device_id={"dp": neighbour(to, dy, 0, 0)}, device_id_type=MESH)

    def w_copy(j):
        to = in_turn(d, j)
        return pltpu.make_async_remote_copy(
            src_ref=w_ref, dst_ref=rows_of_w,
            send_sem=w_send.at[j], recv_sem=w_recv.at[j],
            device_id={"dp": to}, device_id_type=MESH)

    def owner(i, mine):
        return in_turn(d, i + blocks * jnp.where(mine, h, 1 - h))

    def other_copy(i):
        return pltpu.make_async_remote_copy(
            src_ref=back_hbm.at[:, columns(owner(i, False))], dst_ref=bufs.at[OTHER, i],
            send_sem=other_send.at[i], recv_sem=other_recv.at[i],
            device_id={"section": pair}, device_id_type=MESH)

    def chain_copy(i, part):
        k, rows = i * ROW_PARTS + part, pl.ds(part * size, size)
        return pltpu.make_async_remote_copy(
            src_ref=bufs.at[NEXT, i, rows], dst_ref=bufs.at[SUM, i, rows],
            send_sem=chain_send.at[k], recv_sem=chain_recv.at[k],
            device_id={"section": below}, device_id_type=MESH)

    def pair_copy(i, to):
        return pltpu.make_async_remote_copy(
            src_ref=bufs.at[GRAD + 1 - h, i], dst_ref=rows_of_grad,
            send_sem=pair_send.at[i], recv_sem=pair_recv.at[i],
            device_id={"section": pair, "dp": to}, device_id_type=MESH)

    def same_copy(i, to):
        return pltpu.make_async_remote_copy(
            src_ref=bufs.at[GRAD + h, i], dst_ref=rows_of_grad,
            send_sem=same_send.at[i], recv_sem=same_recv.at[i],
            device_id={"dp": to}, device_id_type=MESH)

    def remote(i):
        return (h == 0) | (i < blocks - 1)

    own_ctx = pltpu.make_async_copy(ctx_ref.at[:, columns(d)], rows_of_ctx, own_sem.at[2])
    own_w = pltpu.make_async_copy(w_ref, rows_of_w, own_sem.at[3])
    own_grad = pltpu.make_async_copy(bufs.at[GRAD + 1, blocks - 1], rows_of_grad, own_sem.at[4])

    @pl.loop(0, blocks)
    def _(i):
        other_copy(i).start()

    own_pass = pltpu.make_async_copy(ctx_ref.at[:, columns(across)], rows_to_pass, own_sem.at[5])
    own_ctx.start()
    own_w.start()
    own_pass.start()

    def send_ctx(j):
        w_copy(j).start()

        @pl.when(jnp.where(lower, over_y(j) == 0, j != PARTNER_TURN))
        def _():
            ctx_copy(j).start()

    head = z == levels - 1

    @pl.when(jnp.logical_not(head))
    def _():
        pl.loop(0, last)(send_ctx)

    for load in loads:
        load.wait()

    @pl.when(lower)
    def _():
        @pl.loop(0, blocks)
        def _(i):
            other_copy(i).wait_send()

        @pl.loop(0, last)
        def _(j):
            @pl.when(over_y(j) == 1)
            def _():
                ctx_copy(j).start()

    later = jnp.where(z < levels // 2, -blocks, z - 1)

    def finished(i):
        return jnp.clip(2 * (i - later), 0, i)

    def finish(i):
        to = owner(i, True)
        cols = columns(to)
        odd = bufs[SUM, i].astype(jnp.float32) + top_ref[:, cols].astype(jnp.float32)
        bufs[GRAD + 1, i] = odd.astype(jnp.bfloat16)

        @pl.when(h == 0)
        def _():
            bufs[GRAD, i] = (odd + bufs[OTHER, i].astype(jnp.float32)).astype(jnp.bfloat16)

        @pl.when(h == 1)
        def _():
            bufs[GRAD, i] = (odd + back_ref[:, cols].astype(jnp.float32)).astype(jnp.bfloat16)

        pair_copy(i, to).start()

        @pl.when(remote(i))
        def _():
            same_copy(i, to).start()

    @pl.loop(0, blocks)
    def _(i):
        cols = columns(owner(i, True))
        other_copy(i).wait_recv()
        for part in range(ROW_PARTS):
            rows = pl.ds(part * size, size)

            @pl.when(z < levels - 1)
            def _():
                chain_copy(i, part).wait_recv()

            @pl.when(z > 0)
            def _():
                here = back_ref[rows, cols].astype(jnp.float32) + bufs[OTHER, i, rows, :].astype(jnp.float32)
                bufs[NEXT, i, rows, :] = (bufs[SUM, i, rows, :].astype(jnp.float32) + here).astype(jnp.bfloat16)
                chain_copy(i, part).start()

        @pl.when(head)
        def _():
            send_ctx(2 * i)

            @pl.when(i < blocks - 1)
            def _():
                send_ctx(2 * i + 1)

        pl.loop(finished(i), finished(i + 1))(finish)

    pl.loop(finished(blocks), blocks)(finish)

    @pl.when(h == 1)
    def _():
        own_grad.start()

    @pl.loop(0, blocks)
    def _(i):
        @pl.when(jnp.logical_not(lower))
        def _():
            other_copy(i).wait_send()

        @pl.when(z > 0)
        def _():
            for part in range(ROW_PARTS):
                chain_copy(i, part).wait_send()

        pair_copy(i, d).wait()

        @pl.when(remote(i))
        def _():
            same_copy(i, owner(i, True)).wait()

    @pl.loop(0, last)
    def _(j):
        w_copy(j).wait()

        @pl.when(lower | (j != PARTNER_TURN))
        def _():
            ctx_copy(j).wait()

    own_ctx.wait()
    own_w.wait()
    own_pass.wait()

    @pl.when(h == 1)
    def _():
        own_grad.wait()


def suffix_and_columns(back, top, ctx, token_batch, plan, sections, owners):
    rows, width = ctx.shape
    dma = pltpu.SemaphoreType.DMA
    blocks = owners // 2
    return pl.pallas_call(
        functools.partial(suffix_kernel, sections, owners),
        out_shape=jax.ShapeDtypeStruct((3, owners, rows + W_ROWS, BLK), jnp.bfloat16),
        in_specs=[pl.BlockSpec(memory_space=pltpu.HBM)] * 3 + [
            pl.BlockSpec(memory_space=pltpu.VMEM),
            pl.BlockSpec(memory_space=pltpu.SMEM),
        ],
        out_specs=pl.BlockSpec(memory_space=pl.ANY),
        scratch_shapes=[
            pltpu.VMEM((rows, width), jnp.bfloat16),
            pltpu.VMEM((rows, width), jnp.bfloat16),
            pltpu.VMEM((W_ROWS, rows), jnp.bfloat16),
            pltpu.VMEM((5, blocks, rows, BLK), jnp.bfloat16),
        ] + [dma((blocks,))] * 2 + [dma((blocks * ROW_PARTS,))] * 2 + [dma((blocks,))] * 4
        + [dma((owners,))] * 4 + [dma((6,))],
        compiler_params=pltpu.CompilerParams(
            collective_id=0, has_side_effects=True, vmem_limit_bytes=54 * MIB),
        cost_estimate=pl.CostEstimate(flops=10 ** 7, bytes_accessed=10 ** 7, transcendentals=0),
    )(back, top, ctx, token_batch.reshape(1, rows), plan)


def split(x):
    high = x.astype(jnp.bfloat16)
    return high, (x - high.astype(jnp.float32)).astype(jnp.bfloat16)


def mm(a, b):
    return jnp.dot(a, b, preferred_element_type=jnp.float32)


PIECES = 4


def eye_block():
    rows = lax.broadcasted_iota(jnp.int32, (BLK, BLK), 0)
    return (rows == lax.broadcasted_iota(jnp.int32, (BLK, BLK), 1)).astype(jnp.float32)


def spectrum(squared):
    sums = jnp.sum(jnp.abs(squared), axis=0, keepdims=True)
    return jnp.sqrt(jnp.max(sums, axis=1, keepdims=True)) * 1.001


def first_steps(a, squared):
    top = spectrum(squared)
    reach = (top - damping) / (top + damping)
    scale = 2.0 / (top + damping)
    grow = 2.0 / (2.0 - reach * reach)
    eye = eye_block()
    inv = grow * (2.0 * scale * eye - (scale * scale) * a)
    residual = eye - grow * (2.0 * scale * a - (scale * scale) * squared)
    return inv, residual, after(reach)


def after(reach):
    return reach * reach / (2.0 - reach * reach)


def exact(a, b):
    return jnp.dot(a, b, precision=lax.Precision.HIGHEST, preferred_element_type=jnp.float32)


def inverse_kernel(
    tokens, owned, pre_ref,
    parts_ref, w_ref, weighted, mat, inv, mat_left, inv_left, inv_right, twice, sems,
):
    owners, tile, _ = parts_ref.shape
    eye = eye_block()
    piece = owners // PIECES
    loads = []
    for k in range(PIECES):
        some = pl.ds(k * piece, piece)
        loads.append((
            pltpu.make_async_copy(
                owned.at[0, some, pl.ds(0, tile)], parts_ref.at[some], sems.at[0, k]),
            pltpu.make_async_copy(
                owned.at[1, some, pl.ds(tile, W_ROWS), pl.ds(0, tile)], w_ref.at[some], sems.at[1, k]),
        ))
        for load in loads[-1]:
            load.start()

    def turn(t):
        at = pl.ds(t * tile, tile)
        w = w_ref[t, 0:1, :].astype(jnp.float32)
        weighted[:, at] = (parts_ref[t].astype(jnp.float32).T * w).astype(jnp.bfloat16)

    for k in range(PIECES):
        for load in loads[k]:
            load.wait()
        for t in range(k * piece, (k + 1) * piece):
            turn(t)

    def put_right(high, low):
        inv_right[0:BLK, :] = high
        inv_right[BLK:2 * BLK, :] = low
        inv_right[2 * BLK:3 * BLK, :] = high

    def put_inverse(x):
        inv[...] = x
        high, low = split(x)
        put_right(high, low)
        inv_left[:, 0:BLK] = high
        inv_left[:, BLK:2 * BLK] = low

    def put_residual(residual):
        residual = residual.astype(jnp.bfloat16)
        twice[0:BLK, :] = residual
        twice[BLK:2 * BLK, :] = residual

    grad = parts_ref[...].reshape(tokens, BLK)
    a = mm(weighted[...], grad) * (1.0 / tokens) + damping * eye
    mat[...] = a
    high, low = split(a)
    mat_left[:, 0:BLK] = high
    mat_left[:, BLK:2 * BLK] = high
    mat_left[:, 2 * BLK:3 * BLK] = low
    put_right(high, low)
    squared = mm(mat_left[...], inv_right[...])
    x, residual, reach = first_steps(a, squared)
    put_inverse(x)
    put_residual(residual)
    reach = jnp.max(reach)
    quick = jnp.max(spectrum(squared)) <= 512.0 * damping

    def quick_update(reach):
        step = mm(inv_left[...], twice[...])
        put_inverse((2.0 / (2.0 - reach * reach)) * (inv[...] + step))
        return after(reach)

    def quick_body(reach):
        put_residual(eye - mm(mat_left[...], inv_right[...]))
        return quick_update(reach)

    def full_body(reach):
        x = inv[...]
        inv[...] = (2.0 / (2.0 - reach * reach)) * (x + exact(x, eye - exact(mat[...], x)))
        return after(reach)

    @pl.when(quick)
    def _():
        lax.while_loop(lambda r: r > 1e-4, quick_body, quick_update(reach))

    @pl.when(jnp.logical_not(quick))
    def _():
        lax.while_loop(lambda r: r > 1e-6, full_body, reach)

    pre_ref[...] = mm(parts_ref[...].reshape(tokens, BLK), inv[...].astype(jnp.bfloat16)).astype(jnp.bfloat16)


def inverses(owned):
    _, owners, tile, _ = owned.shape
    tile = tile - W_ROWS
    tokens = owners * tile
    square = (BLK, BLK)
    return pl.pallas_call(
        functools.partial(inverse_kernel, tokens),
        out_shape=jax.ShapeDtypeStruct((tokens, BLK), jnp.bfloat16),
        in_specs=[pl.BlockSpec(memory_space=pl.ANY)],
        out_specs=pl.BlockSpec(memory_space=pltpu.VMEM),
        scratch_shapes=[
            pltpu.VMEM((owners, tile, BLK), jnp.bfloat16),
            pltpu.VMEM((owners, W_ROWS, tile), jnp.bfloat16),
            pltpu.VMEM((BLK, tokens), jnp.bfloat16),
            pltpu.VMEM(square, jnp.float32),
            pltpu.VMEM(square, jnp.float32),
            pltpu.VMEM((BLK, 3 * BLK), jnp.bfloat16),
            pltpu.VMEM((BLK, 2 * BLK), jnp.bfloat16),
            pltpu.VMEM((3 * BLK, BLK), jnp.bfloat16),
            pltpu.VMEM((2 * BLK, BLK), jnp.bfloat16),
            pltpu.SemaphoreType.DMA((2, PIECES)),
        ],
        compiler_params=pltpu.CompilerParams(vmem_limit_bytes=48 * MIB),
        cost_estimate=pl.CostEstimate(flops=2 * 10 ** 10, bytes_accessed=10 ** 7, transcendentals=0),
    )(owned)


DX = (0, 1, 3, 0, 2, 1, 3, 2)
DY = (0, 0, 0, 1, 0, 1, 1, 1)
CODE_X = sum(v << (2 * p) for p, v in enumerate(DX))
CODE_Y = sum(v << p for p, v in enumerate(DY))


def newton_steps(largest, goal):
    reach, steps = (largest - damping) / (largest + damping), 0
    while reach > goal:
        reach, steps = reach * reach / (2.0 - reach * reach), steps + 1
    return steps


INPUT_STEPS = newton_steps((BLK * 36.0 + damping) * 1.01, 1e-4)


def gather_kernel(
    sections, owners, tokens,
    pre_ref, owned, out_ref,
    held, done, begun, ctx_ref, w_ref, ctx_t, pt_ref, mat, inv,
    send_up, send_down, send_y, send_sib, recv, recv_sib, own_sem, out_sem,
):
    d = lax.axis_index("dp")
    half = tokens // 2
    low, high = (0, half), (half, half)
    quarters = [(k * half // 2, half // 2) for k in range(4)]
    end = tokens // 96 * 16
    before, tail = (half + half // 2, half // 2 - end), (tokens - end, end)
    lower = lax.axis_index("section") < sections // 2

    def place(p, dc):
        if isinstance(p, int):
            return neighbour(d, DY[p], DX[p], dc)
        dx = lax.shift_right_logical(jnp.int32(CODE_X), 2 * p) & 3
        dy = lax.shift_right_logical(jnp.int32(CODE_Y), p) & 1
        return neighbour(d, dy, dx, dc)

    up, down = neighbour(d, 0, 1, 0), neighbour(d, 0, 3, 0)
    across, sibling = neighbour(d, 1, 0, 0), neighbour(d, 0, 0, 1)

    barrier = pltpu.get_barrier_semaphore()
    for other in (up, down, across, sibling):
        pl.semaphore_signal(barrier, inc=1, device_id={"dp": other}, device_id_type=MESH)
    own = pltpu.make_async_copy(pre_ref, held.at[d], own_sem.at[0])
    own.start()
    tile = ctx_ref.shape[1]
    side = owners // 2
    here = pl.ds(pl.multiple_of(d // side * side, side), side)
    loads = [
        pltpu.make_async_copy(owned.at[1, here, pl.ds(0, tile)], ctx_ref.at[here], own_sem.at[1]),
        pltpu.make_async_copy(owned.at[1, :, pl.ds(tile, W_ROWS), pl.ds(0, tile)], w_ref, own_sem.at[2]),
    ]
    ctx_over = pltpu.make_async_remote_copy(
        src_ref=owned.at[2, here, pl.ds(0, tile)], dst_ref=ctx_ref.at[here],
        send_sem=own_sem.at[3], recv_sem=own_sem.at[4],
        device_id={"dp": across}, device_id_type=MESH)
    there = pl.ds(pl.multiple_of((1 - d // side) * side, side), side)
    ctx_here = pltpu.make_async_copy(owned.at[1, there, pl.ds(0, tile)], ctx_ref.at[there], own_sem.at[5])
    for load in loads:
        load.start()
    pl.when(lower)(ctx_here.start)
    pl.semaphore_wait(barrier, 4)
    pl.when(jnp.logical_not(lower))(ctx_over.start)

    started = []
    slot = {low: 0, high: 2, before: 3, tail: 1}
    slot.update((rows, k) for k, rows in enumerate(quarters))
    count = {"up": 0, "down": 0, "across": 0}

    def send(p, part, to, send_sem, recv_sem, where=None):
        rows = pl.ds(*part)
        target = held.at[place(p, 0), rows]
        copy = pltpu.make_async_remote_copy(
            src_ref=pre_ref.at[rows] if p == 0 else target, dst_ref=target,
            send_sem=send_sem, recv_sem=recv_sem,
            device_id={"dp": to}, device_id_type=MESH)
        if where is None:
            copy.start()
        else:
            pl.when(where)(copy.start)
        started.append((copy, where))

    def pass_on(way, p, part, there, where=None):
        to, sems = {"up": (up, send_up), "down": (down, send_down), "across": (across, send_y)}[way]
        send(p, part, to, sems.at[count[way]], recv.at[there, slot[part]], where)
        count[way] += 1

    def to_sibling(p, part):
        send(p, part, sibling, send_sib.at[p, slot[part]], recv_sib.at[p, slot[part]])

    def arrived(p, part, dc=0):
        at = held.at[place(p, dc), pl.ds(*part)]
        sems = recv_sib if dc else recv
        pltpu.make_async_copy(at, at, sems.at[p, slot[part]]).wait()

    def got(p, part):
        arrived(p, part)
        to_sibling(p, part)

    def out_copy(block):
        return pltpu.make_async_copy(done.at[block], out_ref.at[:, columns(block)], out_sem.at[block])

    def finish(block, total):
        done[block] = total.astype(jnp.bfloat16)
        out_copy(block).start()

    def multiply(p, dc):
        block = place(p, dc)
        finish(block, mm(pt_ref[...], held[block]))

    def partial(p, dc, *spans):
        block = place(p, dc)
        return sum(mm(pt_ref[:, a:b], held[block, a:b, :]) for a, b in spans)

    def begin_multiply(p, dc, *spans):
        begun[2 * (p - 5) + dc] = partial(p, dc, *spans)

    def go_on(p, dc, *spans):
        begun[2 * (p - 5) + dc] += partial(p, dc, *spans)

    def end_multiply(p, dc, *spans):
        finish(place(p, dc), begun[2 * (p - 5) + dc] + partial(p, dc, *spans))

    for k in range(2):
        pass_on("up", 0, quarters[k], 2)
        pass_on("down", 0, quarters[2 + k], 1)
    pass_on("across", 0, low, 3)
    pass_on("across", 0, high, 3)
    to_sibling(0, low)
    to_sibling(0, high)
    own.wait()
    for load in loads:
        load.wait()

    arrived(2, quarters[0])
    pass_on("up", 2, quarters[0], 4)
    arrived(1, quarters[2])
    pass_on("down", 1, quarters[2], 4)
    arrived(2, quarters[1])
    pass_on("up", 2, quarters[1], 4)
    pass_on("up", 0, high, 2)
    arrived(1, quarters[3])
    pass_on("down", 1, quarters[3], 4)
    pass_on("down", 0, low, 1)
    for k in range(2):
        to_sibling(2, quarters[k])
        to_sibling(1, quarters[2 + k])
    pl.when(lower)(ctx_here.wait)
    pl.when(jnp.logical_not(lower))(ctx_over.wait)

    @pl.loop(0, owners)
    def _(t):
        at = pl.ds(pl.multiple_of(t * tile, tile), tile)
        turned = ctx_ref[t].astype(jnp.float32).T
        ctx_t[:, at] = turned.astype(jnp.bfloat16)
        pt_ref[:, at] = (turned * w_ref[t, 0:1, :].astype(jnp.float32)).astype(jnp.bfloat16)

    eye = eye_block()
    mat[...] = mm(pt_ref[...], ctx_ref[...].reshape(tokens, BLK)) * (1.0 / tokens) + damping * eye
    x, residual, reach = first_steps(mat[...], exact(mat[...], mat[...]))
    inv[...] = (2.0 / (2.0 - reach * reach)) * (x + exact(x, residual))

    def newton(_, reach):
        x = inv[...]
        inv[...] = (2.0 / (2.0 - reach * reach)) * (x + exact(x, eye - exact(mat[...], x)))
        return after(reach)

    reach = lax.fori_loop(2, 4, newton, after(reach))
    for k in range(2):
        arrived(4, quarters[k])
        pass_on("across", 4, quarters[k], 7)
        arrived(4, quarters[2 + k])
        pass_on("across", 4, quarters[2 + k], 7)
    arrived(3, low)
    pass_on("up", 3, low, 6)
    pass_on("down", 3, low, 5)
    to_sibling(3, low)
    for k in range(4):
        to_sibling(4, quarters[k])

    reach = lax.fori_loop(4, 8, newton, reach)
    arrived(3, high)
    for rows, where in ((quarters[2], None), (before, None), (tail, jnp.logical_not(lower))):
        pass_on("up", 3, rows, 6, where)
        pass_on("down", 3, rows, 5, where)
    to_sibling(3, high)

    lax.fori_loop(8, INPUT_STEPS, newton, reach)
    ahead, behind = split(inv[...])
    rest_of_it = (inv[...] - ahead.astype(jnp.float32) - behind.astype(jnp.float32)).astype(jnp.bfloat16)
    pt_ref[...] = (
        mm(ahead, ctx_t[...]) + (mm(behind, ctx_t[...]) + mm(rest_of_it, ctx_t[...]))).astype(jnp.bfloat16)

    @pl.loop(0, 1)
    def _(p):
        multiply(p, 0)

    @pl.loop(3, 5)
    def _(p):
        multiply(p, 0)

    got(2, high)
    pass_on("across", 1, tail, 5, lower)
    pass_on("across", 2, tail, 6, lower)
    got(1, low)

    @pl.loop(1, 3)
    def _(p):
        multiply(p, 0)

    for rows in (low, high):
        arrived(0, rows, 1)
        arrived(3, rows, 1)
    for k in range(2):
        arrived(1, quarters[2 + k], 1)
        arrived(2, quarters[k], 1)
    for k in range(4):
        arrived(4, quarters[k], 1)
    arrived(1, low, 1)
    arrived(2, high, 1)

    @pl.loop(0, 5)
    def _(p):
        multiply(p, 1)

    got(5, low)
    got(6, low)
    got(7, quarters[0])
    got(7, quarters[2])
    soon = (0, half // 2), (half, half + half // 2)
    late = (half // 2, half), (half + half // 2, tokens)
    for dc in range(2):
        if dc:
            arrived(5, low, 1)
            arrived(6, low, 1)
            arrived(7, quarters[0], 1)
            arrived(7, quarters[2], 1)
        begin_multiply(5, dc, (0, half))
        begin_multiply(6, dc, (0, half))
        begin_multiply(7, dc, *soon)

    got(5, quarters[2])
    got(6, quarters[2])
    for dc in range(2):
        for p in (5, 6):
            if dc:
                arrived(p, quarters[2], 1)
            go_on(p, dc, (half, half + half // 2))

    got(7, quarters[1])
    got(7, quarters[3])
    for rows in (before, tail):
        got(5, rows)
        got(6, rows)
    for dc in range(2):
        if dc:
            arrived(7, quarters[1], 1)
            arrived(7, quarters[3], 1)
            for rows in (before, tail):
                arrived(5, rows, 1)
                arrived(6, rows, 1)
        end_multiply(7, dc, *late)
        end_multiply(5, dc, (half + half // 2, tokens))
        end_multiply(6, dc, (half + half // 2, tokens))

    for copy, where in started:
        if where is None:
            copy.wait_send()
        else:
            pl.when(where)(copy.wait_send)

    @pl.loop(0, owners)
    def _(block):
        out_copy(block).wait()


def gather_and_multiply(pre, owned):
    tokens = pre.shape[0]
    _, owners, tile, _ = owned.shape
    tile = tile - W_ROWS
    dma = pltpu.SemaphoreType.DMA
    product = pl.pallas_call(
        functools.partial(gather_kernel, lax.axis_size("section"), owners, tokens),
        out_shape=jax.ShapeDtypeStruct((BLK, owners * BLK), jnp.bfloat16),
        in_specs=[pl.BlockSpec(memory_space=pl.ANY)] * 2,
        out_specs=pl.BlockSpec(memory_space=pl.ANY),
        scratch_shapes=[
            pltpu.VMEM((owners, tokens, BLK), jnp.bfloat16),
            pltpu.VMEM((owners, BLK, BLK), jnp.bfloat16),
            pltpu.VMEM((6, BLK, BLK), jnp.float32),
            pltpu.VMEM((owners, tile, BLK), jnp.bfloat16),
            pltpu.VMEM((owners, W_ROWS, tile), jnp.bfloat16),
            pltpu.VMEM((BLK, tokens), jnp.bfloat16),
            pltpu.VMEM((BLK, tokens), jnp.bfloat16),
            pltpu.VMEM((BLK, BLK), jnp.float32),
            pltpu.VMEM((BLK, BLK), jnp.float32),
            dma((9,)), dma((9,)), dma((8,)), dma((8, 4)), dma((8, 4)), dma((8, 4)), dma((6,)), dma((owners,)),
        ],
        compiler_params=pltpu.CompilerParams(
            collective_id=1, has_side_effects=True, vmem_limit_bytes=46 * MIB),
        cost_estimate=pl.CostEstimate(flops=10 ** 10, bytes_accessed=10 ** 7, transcendentals=0),
    )(pre, owned)
    return product * jnp.bfloat16(1.0 / tokens)


def local(context, back_terms, top_grad, token_batch, plan):
    sections, owners = lax.axis_size("section"), lax.axis_size("dp")
    owned = suffix_and_columns(
        back_terms[0], top_grad, context[0], token_batch, plan, sections, owners)
    return gather_and_multiply(inverses(owned), owned)[None]


def solution(mesh):
    return jax.shard_map(
        local,
        mesh=mesh,
        in_specs=(P("section", "dp", None), P("section", "dp", None), P("dp", None), P("dp"), P()),
        out_specs=P("section", "dp", None),
        check_vma=False,
    )
```
